128 devices in a mesh: outer: 8 (over z, core), inner: 16 (over x, y).
Axes of the slice: x: 4, y: 4, z: 4, core: 2. Of those that a mesh axis runs over, the one named last changes fastest.
Arguments:
- signal: float32 [65536, 512], P(('outer', 'inner')), may hold values from -6 to 6
- spectrum: float32 [128, 2, 512, 256], P(('outer', 'inner')), may hold values from -6 to 6
- skip_gain: float32 [512], replicated, may hold values from 0.5 to 1.5
Outputs:
- output: float32 [65536, 512], P(('outer', 'inner'))
The draws below stay inside these ranges and needn't reach their ends.
All inputs are finite; a program needn't handle non-finite values.
Results may differ from the reference program's by a relative error of at most 0.000059.
Values sent between devices are 32-bit elements; how exact they have to be, the bound alone decides.
A program may use at most 64 MiB of HBM per device.

```python
import jax
import jax.numpy as jnp
from jax import lax

C = 512
SEQ_DEV = 512
BLOCKS = 128
SEQ_LEN = 65536
N_OUTER = 8
N_INNER = 16


def levels(own_key, extent, pieces, least, high):
    gain = 1.0
    for position, parts in pieces:
        heights = jax.random.uniform(jax.random.fold_in(jax.random.fold_in(own_key, 6), position), (parts,), jnp.float32, least / len(pieces), high / len(pieces))
        gain = gain * jnp.repeat(jnp.exp(heights), extent[position] // parts).reshape((-1,) + (1,) * (len(extent) - 1 - position))
    return gain


def centred(stream_key, shape, deviation, bound, pieces=(), held_as=jnp.bfloat16):
    result = jax.random.normal(stream_key, shape, jnp.float32) * deviation
    if len(pieces) > 0:
        result = levels(stream_key, shape, pieces, -0.22, 0.18) * result
    return jnp.clip(result, min=-bound, max=bound).astype(held_as)


def setup_inputs(seed: int = 0) -> dict:
    keys = jax.random.split(jax.random.key(seed), 4)
    return {
        "signal": centred(keys[0], (SEQ_LEN, C), 1.0, 6.0, ((0, 128),), jnp.float32),
        "spectrum": centred(keys[1], (BLOCKS, 2, SEQ_DEV, C // 2), 1.0, 6.0, ((0, 128),), jnp.float32),
        "skip_gain": jnp.clip(jax.random.uniform(keys[2], (C,), jnp.float32, 0.5, 1.5), 0.5, 1.5),
    }


def zero_slot_filter(spec_re, spec_im):
    half_len = spec_re.shape[0] // 2
    low_re = spec_re[1:half_len]
    low_im = spec_im[1:half_len]
    top_re = spec_re[half_len:]
    top_im = spec_im[half_len:]
    zero_row = jnp.zeros_like(spec_re[:1])
    base_re = jnp.concatenate([spec_re[:1], low_re, spec_im[:1], low_re[::-1]], 0)
    base_im = jnp.concatenate([zero_row, low_im, zero_row, -low_im[::-1]], 0)
    mid_re = jnp.concatenate([top_re, top_re[::-1]], 0)
    mid_im = jnp.concatenate([top_im, -top_im[::-1]], 0)
    return base_re, base_im, mid_re, mid_im


def reference(signal, spectrum, skip_gain):
    blocks = N_OUTER * N_INNER
    slot_count = blocks // 2
    seq_total = SEQ_DEV * blocks
    half_chan = C // 2
    packed = spectrum.reshape(slot_count, 2, 2, SEQ_DEV, half_chan)
    packed = packed.transpose(0, 2, 3, 1, 4).reshape(slot_count, 2, SEQ_DEV, C)
    block_width = 32
    block_count = C // block_width

    def one_block(index):
        start = index * block_width
        part_spec = lax.dynamic_slice_in_dim(packed, start, block_width, 3)
        part_sig = lax.dynamic_slice_in_dim(signal, start, block_width, 1)
        part_gain = lax.dynamic_slice_in_dim(skip_gain, start, block_width, 0)
        base_re, base_im, mid_re, mid_im = zero_slot_filter(part_spec[0, 0], part_spec[0, 1])
        middle = part_spec[1:, 0] + 1j * part_spec[1:, 1]
        mirror = jnp.conj(middle[::-1, ::-1])
        columns = jnp.concatenate([(base_re + 1j * base_im)[None], middle, (mid_re + 1j * mid_im)[None], mirror], 0)
        response = columns.transpose(1, 0, 2).reshape(seq_total, block_width)
        forward = jnp.fft.fft(part_sig, axis=0)
        conv = jnp.real(jnp.fft.ifft(forward * response, axis=0))
        return conv.astype(jnp.float32) + part_gain[None, :] * part_sig

    stacked = lax.map(one_block, jnp.arange(block_count, dtype=jnp.int32))
    return stacked.transpose(1, 0, 2).reshape(seq_total, C).astype(jnp.float32)
```

```python
import functools
import math

import jax
import jax.numpy as jnp
import ml_dtypes
import numpy as np
from jax import lax
from jax.experimental import pallas as pl
from jax.experimental.pallas import tpu as pltpu
from jax.sharding import PartitionSpec as P

F32 = jnp.float32
BF16 = jnp.bfloat16
LANES = 128
STEP = 21


def halves(table):
    high = table.astype(ml_dtypes.bfloat16)
    low = (table - high.astype(np.float64)).astype(ml_dtypes.bfloat16)
    return high, low


def tables(blocks, seq_len):
    slots = blocks // 2
    total = blocks * seq_len
    d = np.arange(blocks)
    s = np.arange(slots)
    m = np.arange(seq_len)
    angle = 2.0 * math.pi / blocks * (s[:, None] * d[None, :] % blocks)
    cos_rows = np.cos(angle)
    sin_rows = np.sin(angle)
    sin_rows[0] = np.where(d % 2 == 0, -1.0, 1.0)
    fwd = np.concatenate([cos_rows, -sin_rows], 0)
    scale = np.where(s == 0, 1.0, 2.0)[:, None] / total
    minus = sin_rows * scale
    minus[0] = np.where(d % 2 == 0, 1.0, -1.0) * scale[0]
    inv = np.concatenate([cos_rows * scale, minus], 0).T
    turn = 2.0 * math.pi / total * (np.arange(slots + 1)[:, None] * m[None, :] % total)
    twiddle = np.stack([np.cos(turn[:slots]), np.sin(turn[:slots])]).astype(np.float32)
    middle = np.stack([np.cos(turn[slots]), np.sin(turn[slots])]).astype(np.float32)
    middle = np.concatenate([middle, np.zeros((6, seq_len), np.float32)], 0)
    theta = 2.0 * math.pi / seq_len * (m[:, None] * m[None, :] % seq_len)
    cos_t = np.cos(theta)
    sin_t = np.sin(theta)
    dft = np.concatenate(
        [np.concatenate([cos_t, -sin_t], 1), np.concatenate([sin_t, cos_t], 1)], 0
    )
    fwd_hl = np.stack(halves(fwd))
    inv_hl = np.stack(halves(inv))
    dft_hl = np.stack(halves(dft))
    return fwd_hl, inv_hl, dft_hl, twiddle, middle


def split(value):
    high = value.astype(BF16)
    return high, (value - high.astype(F32)).astype(BF16)


def mm(left, right):
    return jnp.dot(left, right, preferred_element_type=F32)


def table_dot(table_ref, value):
    high, low = split(value)
    return mm(table_ref[0], high) + mm(table_ref[0], low) + mm(table_ref[1], high)


def dft_dot(rows, dft_ref):
    high, low = split(rows)
    return mm(high, dft_ref[0]) + mm(low, dft_ref[0]) + mm(high, dft_ref[1])


def kernel(
    blocks,
    inner,
    signal_hbm,
    spectrum_hbm,
    dft_hbm,
    fwd_hbm,
    inv_hbm,
    twiddle_hbm,
    middle_hbm,
    out_ref,
    signal,
    spectrum,
    dft,
    fwd,
    inv,
    twiddle,
    middle,
    send_x,
    recv_x,
    send_f,
    recv_f,
    send_y,
    recv_y,
    stack,
    bins,
    load_sem,
    x_sem,
    f_sem,
    y_sem,
):
    me = lax.axis_index("outer") * inner + lax.axis_index("inner")
    slots = blocks // 2
    seq_len = signal.shape[0]
    m_tiles = seq_len // LANES
    half_rows = stack.shape[0] // 2

    loads = []
    for i, (src, dst) in enumerate(
        (
            (signal_hbm, signal),
            (spectrum_hbm, spectrum),
            (fwd_hbm, fwd),
            (twiddle_hbm, twiddle),
            (middle_hbm, middle),
            (dft_hbm, dft),
            (inv_hbm, inv),
        )
    ):
        copy = pltpu.make_async_copy(src, dst, load_sem.at[i])
        copy.start()
        loads.append(copy)

    def partner(k):
        p = lax.rem(me + lax.rem(k * STEP, blocks), blocks)
        return p, (p // inner, lax.rem(p, inner))

    barrier = pltpu.get_barrier_semaphore()

    @pl.loop(1, blocks)
    def _(k):
        _, device = partner(k)
        pl.semaphore_signal(
            barrier, inc=1, device_id=device, device_id_type=pl.DeviceIdType.MESH
        )

    def exchange(src, dst, rows, sems):
        @pl.loop(1, blocks)
        def _(k):
            p, device = partner(k)
            pltpu.make_async_remote_copy(
                src_ref=src.at[pl.ds(pl.multiple_of(p * rows, rows), rows)],
                dst_ref=dst.at[pl.ds(pl.multiple_of(me * rows, rows), rows)],
                send_sem=sems.at[0],
                recv_sem=sems.at[1],
                device_id=device,
                device_id_type=pl.DeviceIdType.MESH,
            ).start()

        own = pl.ds(pl.multiple_of(me * rows, rows), rows)
        dst[own, :] = src[own, :]

    def wait_all(ref, rows, sem):
        part = ref.at[pl.ds(0, (blocks - 1) * rows)]
        pltpu.make_async_copy(part, part, sem).wait()

    loads[0].wait()
    chan_tiles = signal.shape[1] // LANES
    x_rows = chan_tiles * m_tiles
    for ct in range(chan_tiles):
        for mt in range(m_tiles):
            tile = signal[mt * LANES : (mt + 1) * LANES, ct * LANES : (ct + 1) * LANES]
            send_x[pl.ds(ct * m_tiles + mt, LANES, stride=x_rows), :] = tile.T
    pl.semaphore_wait(barrier, blocks - 1)
    exchange(send_x, recv_x, x_rows, x_sem)

    loads[1].wait()
    f_rows = 2 * m_tiles
    for g in range(2):
        for r in range(2):
            for bt in range(m_tiles):
                tile = spectrum[
                    r, bt * LANES : (bt + 1) * LANES, g * LANES : (g + 1) * LANES
                ]
                send_f[g, pl.ds(r * m_tiles + bt, LANES, stride=f_rows), :] = tile.T
        exchange(send_f.at[g], recv_f.at[g], f_rows, f_sem.at[g])

    for copy in loads[2:]:
        copy.wait()
    first = lax.broadcasted_iota(jnp.int32, (slots, seq_len), 0) == 0

    wait_all(recv_x, x_rows, x_sem.at[1])
    for g in range(2):
        base = g * half_rows
        extra = []
        for h in range(2):
            ct = 2 * h + g
            data = jnp.concatenate(
                [
                    recv_x[pl.ds(ct * m_tiles + mt, blocks, stride=x_rows), :]
                    for mt in range(m_tiles)
                ],
                1,
            )
            packed = table_dot(fwd, data)
            re = packed[:slots]
            im = packed[slots:]
            cos_t = twiddle[0]
            sin_t = twiddle[1]
            rows = pl.ds(base + h * slots, slots)
            stack[rows, :seq_len] = re * cos_t + im * sin_t
            stack[rows, seq_len:] = jnp.where(first, 0.0, im * cos_t - re * sin_t)
            extra.append(im[0:1])
        pad = jnp.zeros((half_rows - 2 * slots - 2, seq_len), F32)
        middle_in = jnp.concatenate([*extra, pad], 0)
        rows = pl.ds(base + 2 * slots, half_rows - 2 * slots)
        stack[rows, :seq_len] = middle_in * middle[0:1]
        stack[rows, seq_len:] = -middle_in * middle[1:2]
    bins[...] = dft_dot(stack[...], dft)

    lane = lax.broadcasted_iota(jnp.int32, (1, LANES), 1)
    for g in range(2):
        base = g * half_rows
        wait_all(recv_f.at[g], f_rows, f_sem.at[g, 1])
        mid_re = []
        mid_im = []
        for h in range(2):
            rows = pl.ds(base + h * slots, slots)
            f_re = [
                recv_f[g, pl.ds(h * f_rows + bt, slots, stride=2 * f_rows), :]
                for bt in range(m_tiles)
            ]
            f_im = [
                recv_f[g, pl.ds(h * f_rows + m_tiles + bt, slots, stride=2 * f_rows), :]
                for bt in range(m_tiles)
            ]
            top_re = [t[0:1] for t in f_re]
            top_im = [t[0:1] for t in f_im]
            half = m_tiles // 2
            zero = jnp.zeros((1, LANES), F32)
            base_re = [2.0 * t for t in top_re[:half]] + [zero] * half
            base_im = [2.0 * t for t in top_im[:half]] + [zero] * half
            base_re[0] = jnp.where(lane == 0, top_re[0], base_re[0])
            base_im[0] = jnp.where(lane == 0, 0.0, base_im[0])
            base_re[half] = jnp.where(lane == 0, top_im[0], 0.0)
            mid_re.append(
                jnp.concatenate([2.0 * t for t in top_re[half:]] + [zero] * half, 1)
            )
            mid_im.append(
                jnp.concatenate([2.0 * t for t in top_im[half:]] + [zero] * half, 1)
            )
            f_re = jnp.where(
                first, jnp.concatenate(base_re, 1), jnp.concatenate(f_re, 1)
            )
            f_im = jnp.where(
                first, jnp.concatenate(base_im, 1), jnp.concatenate(f_im, 1)
            )
            x_re = bins[rows, :seq_len]
            x_im = bins[rows, seq_len:]
            stack[rows, :seq_len] = f_re * x_re - f_im * x_im
            stack[rows, seq_len:] = -(f_re * x_im + f_im * x_re)
        pad = jnp.zeros((half_rows - 2 * slots - 2, seq_len), F32)
        f_re = jnp.concatenate([*mid_re, pad], 0)
        f_im = jnp.concatenate([*mid_im, pad], 0)
        rows = pl.ds(base + 2 * slots, half_rows - 2 * slots)
        x_re = bins[rows, :seq_len]
        x_im = bins[rows, seq_len:]
        stack[rows, :seq_len] = f_re * x_re - f_im * x_im
        stack[rows, seq_len:] = -(f_re * x_im + f_im * x_re)

        group = pl.ds(base, half_rows)
        back = dft_dot(stack[group, :], dft)
        tail = back[2 * slots :]
        tail = tail[:, :seq_len] * middle[0:1] + tail[:, seq_len:] * middle[1:2]
        for h in range(2):
            part = back[h * slots : (h + 1) * slots]
            re = part[:, :seq_len]
            im = part[:, seq_len:]
            cos_t = twiddle[0]
            sin_t = twiddle[1]
            v_re = re * cos_t + im * sin_t
            v_im = jnp.where(first, tail[h : h + 1], im * cos_t - re * sin_t)
            conv = table_dot(inv, jnp.concatenate([v_re, v_im], 0))
            for mt in range(m_tiles):
                send_y[g, pl.ds(h * m_tiles + mt, blocks, stride=f_rows), :] = conv[
                    :, mt * LANES : (mt + 1) * LANES
                ]
        exchange(send_y.at[g], recv_y.at[g], f_rows, y_sem.at[g])

    for g in range(2):
        wait_all(recv_y.at[g], f_rows, y_sem.at[g, 1])
        for h in range(2):
            ct = 2 * h + g
            for mt in range(m_tiles):
                tile = recv_y[g, pl.ds(h * m_tiles + mt, blocks, stride=f_rows), :]
                out_ref[
                    mt * LANES : (mt + 1) * LANES, ct * LANES : (ct + 1) * LANES
                ] = tile.T

    wait_all(send_x, x_rows, x_sem.at[0])
    for g in range(2):
        wait_all(send_f.at[g], f_rows, f_sem.at[g, 0])
        wait_all(send_y.at[g], f_rows, y_sem.at[g, 0])


def body(signal, spectrum, skip_gain):
    blocks = lax.axis_size(("outer", "inner"))
    inner = lax.axis_size("inner")
    seq_len, channels = signal.shape
    fwd, inv, dft, twiddle, middle = tables(blocks, seq_len)
    chan_tiles = channels // LANES
    m_tiles = seq_len // LANES
    x_rows = chan_tiles * m_tiles
    f_rows = 2 * m_tiles
    stack_rows = 2 * (blocks + 16)
    vmem = pltpu.VMEM
    dma = pltpu.SemaphoreType.DMA
    any_spec = pl.BlockSpec(memory_space=pl.ANY)
    conv = pl.pallas_call(
        functools.partial(kernel, blocks, inner),
        out_shape=jax.ShapeDtypeStruct(signal.shape, F32),
        in_specs=[any_spec] * 7,
        out_specs=pl.BlockSpec(memory_space=pltpu.VMEM),
        scratch_shapes=[
            vmem(signal.shape, F32),
            vmem(spectrum.shape[1:], F32),
            vmem(dft.shape, BF16),
            vmem(fwd.shape, BF16),
            vmem(inv.shape, BF16),
            vmem(twiddle.shape, F32),
            vmem(middle.shape, F32),
            vmem((blocks * x_rows, LANES), F32),
            vmem((blocks * x_rows, LANES), F32),
            vmem((2, blocks * f_rows, LANES), F32),
            vmem((2, blocks * f_rows, LANES), F32),
            vmem((2, blocks * f_rows, LANES), F32),
            vmem((2, blocks * f_rows, LANES), F32),
            vmem((stack_rows, 2 * seq_len), F32),
            vmem((stack_rows, 2 * seq_len), F32),
            dma((7,)),
            dma((2,)),
            dma((2, 2)),
            dma((2, 2)),
        ],
        compiler_params=pltpu.CompilerParams(
            collective_id=1, has_side_effects=True, vmem_limit_bytes=48 * 2**20
        ),
        cost_estimate=pl.CostEstimate(
            flops=5 * 10**9, bytes_accessed=8 * 2**20, transcendentals=0
        ),
        name="hyena_conv",
    )(
        signal,
        spectrum.reshape(spectrum.shape[1:]),
        dft,
        fwd,
        inv,
        twiddle,
        middle,
    )
    return conv + skip_gain[None, :] * signal


def solution(mesh):
    return jax.shard_map(
        body,
        mesh=mesh,
        in_specs=(P(("outer", "inner"), None), P(("outer", "inner"), None, None, None), P()),
        out_specs=P(("outer", "inner"), None),
        check_vma=False,
    )
```

```python
import functools
import itertools
import math
import random

import jax
import jax.numpy as jnp
import ml_dtypes
import numpy as np
from jax import lax
from jax.experimental import pallas as pl
from jax.experimental.pallas import tpu as pltpu
from jax.sharding import PartitionSpec as P

F32 = jnp.float32
BF16 = jnp.bfloat16
LANES = 128


def halves(table):
    high = table.astype(ml_dtypes.bfloat16)
    low = (table - high.astype(np.float64)).astype(ml_dtypes.bfloat16)
    return high, low


def tables(blocks, seq_len):
    slots = blocks // 2
    total = blocks * seq_len
    d = np.arange(blocks)
    s = np.arange(slots)
    m = np.arange(seq_len)
    angle = 2.0 * math.pi / blocks * (s[:, None] * d[None, :] % blocks)
    cos_rows = np.cos(angle)
    sin_rows = np.sin(angle)
    sin_rows[0] = np.where(d % 2 == 0, -1.0, 1.0)
    fwd = np.concatenate([cos_rows, -sin_rows], 0)
    scale = np.where(s == 0, 1.0, 2.0)[:, None] / total
    minus = sin_rows * scale
    minus[0] = np.where(d % 2 == 0, 1.0, -1.0) * scale[0]
    inv = np.concatenate([cos_rows * scale, minus], 0).T
    turn = 2.0 * math.pi / total * (np.arange(slots + 1)[:, None] * m[None, :] % total)
    twiddle = np.stack([np.cos(turn[:slots]), np.sin(turn[:slots])]).astype(np.float32)
    middle = np.stack([np.cos(turn[slots]), np.sin(turn[slots])]).astype(np.float32)
    middle = np.concatenate([middle, np.zeros((6, seq_len), np.float32)], 0)
    theta = 2.0 * math.pi / seq_len * (m[:, None] * m[None, :] % seq_len)
    cos_t = np.cos(theta)
    sin_t = np.sin(theta)
    dft = np.concatenate(
        [np.concatenate([cos_t, -sin_t], 1), np.concatenate([sin_t, cos_t], 1)], 0
    )
    fwd_hl = np.stack(halves(fwd))
    inv_hl = np.stack(halves(inv))
    dft_hl = np.stack(halves(dft))
    return fwd_hl, inv_hl, dft_hl, twiddle, middle


def split(value):
    high = value.astype(BF16)
    return high, (value - high.astype(F32)).astype(BF16)


def mm(left, right):
    return jnp.dot(left, right, preferred_element_type=F32)


def table_dot(table_ref, value):
    high, low = split(value)
    return mm(table_ref[0], high) + mm(table_ref[0], low) + mm(table_ref[1], high)


def dft_dot(rows, dft_ref):
    high, low = split(rows)
    return mm(high, dft_ref[0]) + mm(low, dft_ref[0]) + mm(high, dft_ref[1])


def offsets(mesh_shape):
    axes = [range(n) for n in mesh_shape]
    every = [o for o in itertools.product(*axes) if any(o)]

    def hops(o):
        z, _, x, y = [min(d, n - d) for d, n in zip(o, mesh_shape)]
        return z + x + y

    random.Random(1).shuffle(every)
    return sorted(every, key=lambda o: -hops(o))


def kernel(
    shape,
    signal_hbm,
    spectrum_hbm,
    dft_hbm,
    fwd_hbm,
    inv_hbm,
    twiddle_hbm,
    middle_hbm,
    out_ref,
    signal,
    spectrum,
    dft,
    fwd,
    inv,
    twiddle,
    middle,
    send_x,
    recv_x,
    send_f,
    recv_f,
    send_y,
    recv_y,
    stack,
    bins,
    load_sem,
    x_sem,
    f_sem,
    y_sem,
):
    n_z, n_core, n_x, n_y = shape
    outer = lax.axis_index("outer")
    inner = lax.axis_index("inner")
    n_outer = n_z * n_core
    n_inner = n_x * n_y
    blocks = n_outer * n_inner
    me = outer * n_inner + inner
    slots = blocks // 2
    seq_len = signal.shape[0]
    m_tiles = seq_len // LANES
    rows = 2 * m_tiles
    stack_rows = stack.shape[1]

    def lanes(tile):
        return pl.ds(tile * LANES, LANES)

    loads = {}

    def load(name, src, dst):
        copy = pltpu.make_async_copy(src, dst, load_sem.at[len(loads)])
        copy.start()
        loads[name] = copy

    for g in range(2):
        for h in range(2):
            where = lanes(2 * h + g)
            load(("x", g, h), signal_hbm.at[:, where], signal.at[:, where])

    barrier = pltpu.get_barrier_semaphore()

    @pl.loop(0, n_outer)
    def _(o):
        for i in range(n_inner):

            @pl.when(jnp.logical_or(o != outer, inner != i))
            def _():
                pl.semaphore_signal(
                    barrier,
                    inc=1,
                    device_id=(o, i),
                    device_id_type=pl.DeviceIdType.MESH,
                )

    for g in range(2):
        load(("f", g), spectrum_hbm.at[:, :, lanes(g)], spectrum.at[:, :, lanes(g)])
    load("fwd", fwd_hbm, fwd)
    load("twiddle", twiddle_hbm, twiddle)
    load("middle", middle_hbm, middle)
    load("dft", dft_hbm, dft)
    load("inv", inv_hbm, inv)

    z, core = outer // n_core, lax.rem(outer, n_core)
    x, y = inner // n_y, lax.rem(inner, n_y)
    at_outer = [
        [lax.rem(z + d, n_z) * n_core + lax.rem(core + e, n_core) for e in range(n_core)]
        for d in range(n_z)
    ]
    at_x = [lax.rem(x + d, n_x) * n_y for d in range(n_x)]
    at_y = [lax.rem(y + d, n_y) for d in range(n_y)]
    order = offsets(shape)

    def block(ref, index):
        return ref.at[pl.ds(pl.multiple_of(index * rows, rows), rows)]

    def exchange(src, dst, sems):
        for dz, dc, dx, dy in order:
            to = (at_outer[dz][dc], at_x[dx] + at_y[dy])
            pltpu.make_async_remote_copy(
                src_ref=block(src, to[0] * n_inner + to[1]),
                dst_ref=block(dst, me),
                send_sem=sems.at[0],
                recv_sem=sems.at[1],
                device_id=to,
                device_id_type=pl.DeviceIdType.MESH,
            ).start()
        own = pl.ds(pl.multiple_of(me * rows, rows), rows)
        dst[own, :] = src[own, :]

    def wait_all(ref, sem):
        part = ref.at[pl.ds(0, (blocks - 1) * rows)]
        pltpu.make_async_copy(part, part, sem).wait()

    def spread(ref, g, index, tile):
        ref[g, pl.ds(index, blocks, stride=rows), :] = tile

    for g in range(2):
        for h in range(2):
            loads["x", g, h].wait()
            for mt in range(m_tiles):
                spread(send_x, g, h * m_tiles + mt, signal[lanes(mt), lanes(2 * h + g)].T)
        if g == 0:
            pl.semaphore_wait(barrier, blocks - 1)
        exchange(send_x.at[g], recv_x.at[g], x_sem.at[g])
        loads["f", g].wait()
        for r in range(2):
            for bt in range(m_tiles):
                spread(send_f, g, r * m_tiles + bt, spectrum[r, lanes(bt), lanes(g)].T)
        exchange(send_f.at[g], recv_f.at[g], f_sem.at[g])

    for name in ("fwd", "twiddle", "middle", "dft", "inv"):
        loads[name].wait()
    first = lax.broadcasted_iota(jnp.int32, (slots, seq_len), 0) == 0
    lane = lax.broadcasted_iota(jnp.int32, (1, LANES), 1)
    last_rows = pl.ds(2 * slots, stack_rows - 2 * slots)
    pad = jnp.zeros((stack_rows - 2 * slots - 2, seq_len), F32)

    def forward(g):
        extra = []
        for h in range(2):
            data = jnp.concatenate(
                [
                    recv_x[g, pl.ds(h * m_tiles + mt, blocks, stride=rows), :]
                    for mt in range(m_tiles)
                ],
                1,
            )
            packed = table_dot(fwd, data)
            re = packed[:slots]
            im = packed[slots:]
            cos_t = twiddle[0]
            sin_t = twiddle[1]
            at = pl.ds(h * slots, slots)
            stack[g, at, :seq_len] = re * cos_t + im * sin_t
            stack[g, at, seq_len:] = jnp.where(first, 0.0, im * cos_t - re * sin_t)
            extra.append(im[0:1])
        middle_in = jnp.concatenate([*extra, pad], 0)
        stack[g, last_rows, :seq_len] = middle_in * middle[0:1]
        stack[g, last_rows, seq_len:] = -middle_in * middle[1:2]
        bins[g] = dft_dot(stack[g], dft)

    def times_filter(g, at, f_re, f_im):
        x_re = bins[g, at, :seq_len]
        x_im = bins[g, at, seq_len:]
        stack[g, at, :seq_len] = f_re * x_re - f_im * x_im
        stack[g, at, seq_len:] = -(f_re * x_im + f_im * x_re)

    def backward(g):
        mid_re = []
        mid_im = []
        for h in range(2):
            f_re, f_im = [
                [
                    recv_f[
                        g, pl.ds((h * 2 + r) * m_tiles + bt, slots, stride=2 * rows), :
                    ]
                    for bt in range(m_tiles)
                ]
                for r in range(2)
            ]
            top_re = [t[0:1] for t in f_re]
            top_im = [t[0:1] for t in f_im]
            half = m_tiles // 2
            zero = jnp.zeros((1, LANES), F32)
            base_re = [2.0 * t for t in top_re[:half]] + [zero] * half
            base_im = [2.0 * t for t in top_im[:half]] + [zero] * half
            base_re[0] = jnp.where(lane == 0, top_re[0], base_re[0])
            base_im[0] = jnp.where(lane == 0, 0.0, base_im[0])
            base_re[half] = jnp.where(lane == 0, top_im[0], 0.0)
            mid_re.append(
                jnp.concatenate([2.0 * t for t in top_re[half:]] + [zero] * half, 1)
            )
            mid_im.append(
                jnp.concatenate([2.0 * t for t in top_im[half:]] + [zero] * half, 1)
            )
            times_filter(
                g,
                pl.ds(h * slots, slots),
                jnp.where(first, jnp.concatenate(base_re, 1), jnp.concatenate(f_re, 1)),
                jnp.where(first, jnp.concatenate(base_im, 1), jnp.concatenate(f_im, 1)),
            )
        times_filter(
            g,
            last_rows,
            jnp.concatenate([*mid_re, pad], 0),
            jnp.concatenate([*mid_im, pad], 0),
        )
        back = dft_dot(stack[g], dft)
        tail = back[2 * slots :]
        tail = tail[:, :seq_len] * middle[0:1] + tail[:, seq_len:] * middle[1:2]
        for h in range(2):
            part = back[h * slots : (h + 1) * slots]
            re = part[:, :seq_len]
            im = part[:, seq_len:]
            cos_t = twiddle[0]
            sin_t = twiddle[1]
            v_re = re * cos_t + im * sin_t
            v_im = jnp.where(first, tail[h : h + 1], im * cos_t - re * sin_t)
            conv = table_dot(inv, jnp.concatenate([v_re, v_im], 0))
            for mt in range(m_tiles):
                spread(send_y, g, h * m_tiles + mt, conv[:, mt * LANES : (mt + 1) * LANES])

    for g in range(2):
        wait_all(recv_x.at[g], x_sem.at[g, 1])
        forward(g)
        wait_all(recv_f.at[g], f_sem.at[g, 1])
        backward(g)
        exchange(send_y.at[g], recv_y.at[g], y_sem.at[g])

    for g in range(2):
        wait_all(recv_y.at[g], y_sem.at[g, 1])
        for h in range(2):
            for mt in range(m_tiles):
                tile = recv_y[g, pl.ds(h * m_tiles + mt, blocks, stride=rows), :]
                out_ref[lanes(mt), lanes(2 * h + g)] = tile.T

    for g in range(2):
        wait_all(send_x.at[g], x_sem.at[g, 0])
        wait_all(send_f.at[g], f_sem.at[g, 0])
        wait_all(send_y.at[g], y_sem.at[g, 0])


def body(signal, spectrum, skip_gain):
    n_outer = lax.axis_size("outer")
    n_inner = lax.axis_size("inner")
    blocks = n_outer * n_inner
    side = math.isqrt(n_inner)
    shape = (n_outer // 2, 2, side, side)
    seq_len, channels = signal.shape
    fwd, inv, dft, twiddle, middle = tables(blocks, seq_len)
    rows = 2 * (seq_len // LANES)
    vmem = pltpu.VMEM
    dma = pltpu.SemaphoreType.DMA
    in_hbm = pl.BlockSpec(memory_space=pltpu.HBM)
    conv = pl.pallas_call(
        functools.partial(kernel, shape),
        out_shape=jax.ShapeDtypeStruct(signal.shape, F32),
        in_specs=[in_hbm] * 7,
        out_specs=pl.BlockSpec(memory_space=pltpu.VMEM),
        scratch_shapes=[
            vmem(signal.shape, F32),
            vmem(spectrum.shape[1:], F32),
            vmem(dft.shape, BF16),
            vmem(fwd.shape, BF16),
            vmem(inv.shape, BF16),
            vmem(twiddle.shape, F32),
            vmem(middle.shape, F32),
            *[vmem((2, blocks * rows, LANES), F32) for _ in range(6)],
            *[vmem((2, blocks + 16, 2 * seq_len), F32) for _ in range(2)],
            dma((11,)),
            *[dma((2, 2)) for _ in range(3)],
        ],
        compiler_params=pltpu.CompilerParams(
            collective_id=1, has_side_effects=True, vmem_limit_bytes=48 * 2**20
        ),
        cost_estimate=pl.CostEstimate(
            flops=5 * 10**9, bytes_accessed=8 * 2**20, transcendentals=0
        ),
        name="hyena_conv",
    )(
        *[
            pltpu.with_memory_space_constraint(a, pltpu.HBM)
            for a in (
                signal,
                spectrum.reshape(spectrum.shape[1:]),
                dft,
                fwd,
                inv,
                twiddle,
                middle,
            )
        ]
    )
    return conv + skip_gain[None, :] * signal


def solution(mesh):
    return jax.shard_map(
        body,
        mesh=mesh,
        in_specs=(P(("outer", "inner"), None), P(("outer", "inner"), None, None, None), P()),
        out_specs=P(("outer", "inner"), None),
        check_vma=False,
    )
```

```python
import functools
import itertools
import math
import random

import jax
import jax.numpy as jnp
import ml_dtypes
import numpy as np
from jax import lax
from jax.experimental import pallas as pl
from jax.experimental.pallas import tpu as pltpu
from jax.sharding import PartitionSpec as P

F32 = jnp.float32
BF16 = jnp.bfloat16
LANES = 128
RADIX = 4


def halves(table):
    high = table.astype(ml_dtypes.bfloat16)
    low = (table - high.astype(np.float64)).astype(ml_dtypes.bfloat16)
    return high, low


def tables(blocks, seq_len):
    slots = blocks // 2
    total = blocks * seq_len
    d = np.arange(blocks)
    s = np.arange(slots)
    m = np.arange(seq_len)
    angle = 2.0 * math.pi / blocks * (s[:, None] * d[None, :] % blocks)
    cos_rows = np.cos(angle)
    sin_rows = np.sin(angle)
    sin_rows[0] = np.where(d % 2 == 0, -1.0, 1.0)
    fwd = np.concatenate([cos_rows, -sin_rows], 0)
    scale = np.where(s == 0, 1.0, 2.0)[:, None] / total
    inv = (fwd * np.concatenate([scale, scale], 0)).T
    turn = 2.0 * math.pi / total * (np.arange(slots + 1)[:, None] * m[None, :] % total)
    twiddle = np.stack([np.cos(turn[:slots]), np.sin(turn[:slots])]).astype(np.float32)
    middle = np.stack([np.cos(turn[slots]), np.sin(turn[slots])]).astype(np.float32)
    middle = np.concatenate([middle, np.zeros((6, seq_len), np.float32)], 0)
    n = np.arange(LANES)[None, :, None]
    l = np.arange(LANES)[None, None, :]
    r = np.arange(RADIX)[:, None, None]
    theta = 2.0 * math.pi / seq_len * (n * (r + RADIX * l) % seq_len)
    cos_t = np.cos(theta)
    sin_t = np.sin(theta)
    dft = np.concatenate(
        [np.concatenate([cos_t, -sin_t], 2), np.concatenate([sin_t, cos_t], 2)], 1
    )
    dft = np.stack([dft, dft.transpose(0, 2, 1)])
    fwd_hl = np.stack(halves(fwd))
    inv_hl = np.stack(halves(inv))
    dft_hl = np.stack(halves(dft), 1)
    return fwd_hl, inv_hl, dft_hl, twiddle, middle


def split(value):
    high = value.astype(BF16)
    return high, (value - high.astype(F32)).astype(BF16)


def mm(left, right):
    return jnp.dot(left, right, preferred_element_type=F32)


def table_dot(table_ref, value):
    high, low = split(value)
    return mm(table_ref[0], high) + mm(table_ref[0], low) + mm(table_ref[1], high)


def radix4(parts, direction):
    (ar, ai), (br, bi), (cr, ci), (dr, di) = parts
    pr, pi, qr, qi = ar + cr, ai + ci, ar - cr, ai - ci
    sr, si, tr, ti = br + dr, bi + di, br - dr, bi - di
    plus = (qr - ti, qi + tr)
    minus = (qr + ti, qi - tr)
    if direction < 0:
        plus, minus = minus, plus
    return (pr + sr, pi + si), plus, (pr - sr, pi - si), minus


def offsets(mesh_shape):
    axes = [range(n) for n in mesh_shape]
    every = [o for o in itertools.product(*axes) if any(o)]

    def hops(o):
        z, _, x, y = [min(d, n - d) for d, n in zip(o, mesh_shape)]
        return z + x + y

    random.Random(1).shuffle(every)
    return every, sorted(every, key=lambda o: -hops(o))


def kernel(
    shape,
    signal_hbm,
    spectrum_hbm,
    dft_hbm,
    fwd_hbm,
    inv_hbm,
    twiddle_hbm,
    middle_hbm,
    out_ref,
    signal,
    spectrum,
    dft,
    fwd,
    inv,
    twiddle,
    middle,
    send_x,
    recv_x,
    send_f,
    recv_f,
    send_y,
    recv_y,
    parts,
    bins,
    back,
    load_sem,
    x_sem,
    f_sem,
    y_sem,
):
    n_z, n_core, n_x, n_y = shape
    outer = lax.axis_index("outer")
    inner = lax.axis_index("inner")
    n_outer = n_z * n_core
    n_inner = n_x * n_y
    blocks = n_outer * n_inner
    me = outer * n_inner + inner
    slots = blocks // 2
    seq_len = signal.shape[0]
    m_tiles = seq_len // LANES
    rows = 2 * m_tiles
    lines = bins.shape[2]

    def lanes(tile):
        return pl.ds(tile * LANES, LANES)

    loads = {}

    def load(name, src, dst):
        copy = pltpu.make_async_copy(src, dst, load_sem.at[len(loads)])
        copy.start()
        loads[name] = copy

    for g in range(2):
        for h in range(2):
            where = lanes(2 * h + g)
            load(("x", g, h), signal_hbm.at[:, where], signal.at[:, where])

    barrier = pltpu.get_barrier_semaphore()

    @pl.loop(0, n_outer)
    def _(o):
        for i in range(n_inner):

            @pl.when(jnp.logical_or(o != outer, inner != i))
            def _():
                pl.semaphore_signal(
                    barrier,
                    inc=1,
                    device_id=(o, i),
                    device_id_type=pl.DeviceIdType.MESH,
                )

    for g in range(2):
        load(("f", g), spectrum_hbm.at[:, :, lanes(g)], spectrum.at[g])
    load("fwd", fwd_hbm, fwd)
    load("twiddle", twiddle_hbm, twiddle)
    load("middle", middle_hbm, middle)
    load("dft", dft_hbm, dft)
    load("inv", inv_hbm, inv)

    z, core = outer // n_core, lax.rem(outer, n_core)
    x, y = inner // n_y, lax.rem(inner, n_y)
    at_outer = [
        [lax.rem(z + d, n_z) * n_core + lax.rem(core + e, n_core) for e in range(n_core)]
        for d in range(n_z)
    ]
    at_x = [lax.rem(x + d, n_x) * n_y for d in range(n_x)]
    at_y = [lax.rem(y + d, n_y) for d in range(n_y)]
    mixed, far = offsets(shape)

    def block(ref, index):
        return ref.at[pl.ds(pl.multiple_of(index * rows, rows), rows)]

    def exchange(src, dst, sems, order):
        for dz, dc, dx, dy in order:
            to = (at_outer[dz][dc], at_x[dx] + at_y[dy])
            pltpu.make_async_remote_copy(
                src_ref=block(src, to[0] * n_inner + to[1]),
                dst_ref=block(dst, me),
                send_sem=sems.at[0],
                recv_sem=sems.at[1],
                device_id=to,
                device_id_type=pl.DeviceIdType.MESH,
            ).start()
        own = pl.ds(pl.multiple_of(me * rows, rows), rows)
        dst[own, :] = src[own, :]

    def wait_all(ref, sem):
        part = ref.at[pl.ds(0, (blocks - 1) * rows)]
        pltpu.make_async_copy(part, part, sem).wait()

    def spread(ref, g, index, tile):
        ref[g, pl.ds(index, blocks, stride=rows), :] = tile

    for g in range(2):
        for h in range(2):
            loads["x", g, h].wait()
            for mt in range(m_tiles):
                spread(send_x, g, h * m_tiles + mt, signal[lanes(mt), lanes(2 * h + g)].T)
        if g == 0:
            pl.semaphore_wait(barrier, blocks - 1)
        exchange(send_x.at[g], recv_x.at[g], x_sem.at[g], mixed)
        loads["f", g].wait()
        for r in range(2):
            for q in range(RADIX):
                every = pl.ds(q, LANES, stride=RADIX)
                spread(send_f, g, r * m_tiles + q, spectrum[g, r, every, :].T)
        exchange(send_f.at[g], recv_f.at[g], f_sem.at[g], (mixed, far)[g])

    for name in ("fwd", "twiddle", "middle", "dft", "inv"):
        loads[name].wait()
    first = lax.broadcasted_iota(jnp.int32, (slots, LANES), 0) == 0
    lane = lax.broadcasted_iota(jnp.int32, (1, LANES), 1)
    extra_rows = lines - 2 * slots
    pad = jnp.zeros((extra_rows - 2, LANES), F32)
    tiles = [slice(p * LANES, (p + 1) * LANES) for p in range(RADIX)]

    def put(p, at, count, re, im):
        value = jnp.concatenate([re, im], 1)
        high, low = split(value)
        parts[p, pl.ds(at, count), :] = high
        parts[p, pl.ds(lines + at, count), :] = low

    def transform(p, way):
        whole = mm(parts[p], dft[way, 0, p])
        rest = mm(parts[p, :lines], dft[way, 1, p])
        return whole[:lines] + whole[lines:] + rest

    def forward(g):
        extra = []

        def lines_in(at, count, pairs):
            for p, (re, im) in enumerate(radix4(pairs, -1)):
                put(p, at, count, re, im)

        for h in range(2):
            data = jnp.concatenate(
                [
                    recv_x[g, pl.ds(h * m_tiles + mt, blocks, stride=rows), :]
                    for mt in range(m_tiles)
                ],
                1,
            )
            packed = table_dot(fwd, data)
            extra.append(packed[slots : slots + 1])
            pairs = []
            for t in tiles:
                re = packed[:slots, t]
                im = packed[slots:, t]
                cos_t = twiddle[0, :, t]
                sin_t = twiddle[1, :, t]
                pairs.append(
                    (
                        re * cos_t + im * sin_t,
                        jnp.where(first, 0.0, im * cos_t - re * sin_t),
                    )
                )
            lines_in(h * slots, slots, pairs)
        pairs = []
        for t in tiles:
            value = jnp.concatenate([extra[0][:, t], extra[1][:, t], pad], 0)
            pairs.append((value * middle[0:1, t], -value * middle[1:2, t]))
        lines_in(2 * slots, extra_rows, pairs)
        for p in range(RADIX):
            bins[g, p] = transform(p, 0)

    def times_filter(g, p, at, count, f_re, f_im):
        x_re = bins[g, p, pl.ds(at, count), :LANES]
        x_im = bins[g, p, pl.ds(at, count), LANES:]
        put(p, at, count, f_re * x_re - f_im * x_im, f_re * x_im + f_im * x_re)

    def backward(g):
        lower = lane < LANES // 2
        for p in range(RADIX):
            mid = []
            for h in range(2):
                f_re, f_im = [
                    recv_f[
                        g, pl.ds((h * 2 + r) * m_tiles + p, slots, stride=2 * rows), :
                    ]
                    for r in range(2)
                ]
                top_re = f_re[0:8]
                top_im = f_im[0:8]
                far_re = pltpu.roll(top_re, LANES // 2, 1)[0:1]
                far_im = pltpu.roll(top_im, LANES // 2, 1)[0:1]
                top_re = top_re[0:1]
                top_im = top_im[0:1]
                mid.append(
                    (
                        jnp.where(lower, 2.0 * far_re, 0.0),
                        jnp.where(lower, 2.0 * far_im, 0.0),
                    )
                )
                base_re = jnp.where(lower, 2.0 * top_re, 0.0)
                base_im = jnp.where(lower, 2.0 * top_im, 0.0)
                if p == 0:
                    base_re = jnp.where(lane == 0, top_re, base_re)
                    base_re = jnp.where(lane == LANES // 2, far_im, base_re)
                    base_im = jnp.where(lane == 0, 0.0, base_im)
                times_filter(
                    g,
                    p,
                    h * slots,
                    slots,
                    jnp.where(first, base_re, f_re),
                    jnp.where(first, base_im, f_im),
                )
            times_filter(
                g,
                p,
                2 * slots,
                extra_rows,
                jnp.concatenate([mid[0][0], mid[1][0], pad], 0),
                jnp.concatenate([mid[0][1], mid[1][1], pad], 0),
            )
        for p in range(RADIX):
            back[p] = transform(p, 1)

        def lines_out(at, count):
            at = pl.ds(at, count)
            return radix4([(back[p, at, :LANES], back[p, at, LANES:]) for p in range(RADIX)], 1)

        tail = [
            re * middle[0:1, t] - im * middle[1:2, t]
            for t, (re, im) in zip(tiles, lines_out(2 * slots, extra_rows))
        ]
        for h in range(2):
            v_re = []
            v_im = []
            for t, end, (re, im) in zip(tiles, tail, lines_out(h * slots, slots)):
                cos_t = twiddle[0, :, t]
                sin_t = twiddle[1, :, t]
                v_re.append(re * cos_t - im * sin_t)
                v_im.append(jnp.where(first, end[h : h + 1], re * sin_t + im * cos_t))
            value = jnp.concatenate(
                [jnp.concatenate(v_re, 1), jnp.concatenate(v_im, 1)], 0
            )
            conv = table_dot(inv, value)
            for mt in range(m_tiles):
                spread(send_y, g, h * m_tiles + mt, conv[:, tiles[mt]])

    for g in range(2):
        wait_all(recv_x.at[g], x_sem.at[g, 1])
        forward(g)
        wait_all(recv_f.at[g], f_sem.at[g, 1])
        backward(g)
        exchange(send_y.at[g], recv_y.at[g], y_sem.at[g], far)

    for g in range(2):
        wait_all(recv_y.at[g], y_sem.at[g, 1])
        for h in range(2):
            for mt in range(m_tiles):
                tile = recv_y[g, pl.ds(h * m_tiles + mt, blocks, stride=rows), :]
                out_ref[lanes(mt), lanes(2 * h + g)] = tile.T

    for g in range(2):
        wait_all(send_x.at[g], x_sem.at[g, 0])
        wait_all(send_f.at[g], f_sem.at[g, 0])
        wait_all(send_y.at[g], y_sem.at[g, 0])


def body(signal, spectrum, skip_gain):
    n_outer = lax.axis_size("outer")
    n_inner = lax.axis_size("inner")
    blocks = n_outer * n_inner
    side = math.isqrt(n_inner)
    shape = (n_outer // 2, 2, side, side)
    seq_len, channels = signal.shape
    fwd, inv, dft, twiddle, middle = tables(blocks, seq_len)
    rows = 2 * (seq_len // LANES)
    lines = blocks + 16
    vmem = pltpu.VMEM
    dma = pltpu.SemaphoreType.DMA
    in_hbm = pl.BlockSpec(memory_space=pltpu.HBM)
    conv = pl.pallas_call(
        functools.partial(kernel, shape),
        out_shape=jax.ShapeDtypeStruct(signal.shape, F32),
        in_specs=[in_hbm] * 7,
        out_specs=pl.BlockSpec(memory_space=pltpu.VMEM),
        scratch_shapes=[
            vmem(signal.shape, F32),
            vmem((2, 2, seq_len, LANES), F32),
            vmem(dft.shape, BF16),
            vmem(fwd.shape, BF16),
            vmem(inv.shape, BF16),
            vmem(twiddle.shape, F32),
            vmem(middle.shape, F32),
            *[vmem((2, blocks * rows, LANES), F32) for _ in range(6)],
            vmem((RADIX, 2 * lines, 2 * LANES), BF16),
            vmem((2, RADIX, lines, 2 * LANES), F32),
            vmem((RADIX, lines, 2 * LANES), F32),
            dma((11,)),
            *[dma((2, 2)) for _ in range(3)],
        ],
        compiler_params=pltpu.CompilerParams(
            collective_id=1, has_side_effects=True, vmem_limit_bytes=48 * 2**20
        ),
        cost_estimate=pl.CostEstimate(
            flops=2 * 10**9, bytes_accessed=8 * 2**20, transcendentals=0
        ),
        name="hyena_conv",
    )(
        *[
            pltpu.with_memory_space_constraint(a, pltpu.HBM)
            for a in (
                signal,
                spectrum.reshape(spectrum.shape[1:]),
                dft,
                fwd,
                inv,
                twiddle,
                middle,
            )
        ]
    )
    return conv + skip_gain[None, :] * signal


def solution(mesh):
    return jax.shard_map(
        body,
        mesh=mesh,
        in_specs=(P(("outer", "inner"), None), P(("outer", "inner"), None, None, None), P()),
        out_specs=P(("outer", "inner"), None),
        check_vma=False,
    )
```

```python
import functools
import itertools
import math
import random

import jax
import jax.numpy as jnp
import ml_dtypes
import numpy as np
from jax import lax
from jax.experimental import pallas as pl
from jax.experimental.pallas import tpu as pltpu
from jax.sharding import PartitionSpec as P

F32 = jnp.float32
BF16 = jnp.bfloat16
LANES = 128
RADIX = 4


def halves(table):
    high = table.astype(ml_dtypes.bfloat16)
    low = (table - high.astype(np.float64)).astype(ml_dtypes.bfloat16)
    return high, low


def tables(blocks, seq_len):
    slots = blocks // 2
    total = blocks * seq_len
    d = np.arange(blocks)
    s = np.arange(slots)
    m = np.arange(seq_len)
    angle = 2.0 * math.pi / blocks * (s[:, None] * d[None, :] % blocks)
    cos_rows = np.cos(angle)
    sin_rows = np.sin(angle)
    sin_rows[0] = np.where(d % 2 == 0, -1.0, 1.0)
    fwd = np.concatenate([cos_rows, -sin_rows], 0)
    scale = np.where(s == 0, 1.0, 2.0)[:, None] / total
    inv = (fwd * np.concatenate([scale, scale], 0)).T
    turn = 2.0 * math.pi / total * (np.arange(slots + 1)[:, None] * m[None, :] % total)
    twiddle = np.stack([np.cos(turn[:slots]), np.sin(turn[:slots])]).astype(np.float32)
    middle = np.stack([np.cos(turn[slots]), np.sin(turn[slots])]).astype(np.float32)
    middle = np.concatenate([middle, np.zeros((6, seq_len), np.float32)], 0)
    n = np.arange(LANES)[None, :, None]
    l = np.arange(LANES)[None, None, :]
    r = np.arange(RADIX)[:, None, None]
    theta = 2.0 * math.pi / seq_len * (n * (r + RADIX * l) % seq_len)
    cos_t = np.cos(theta)
    sin_t = np.sin(theta)
    dft = np.concatenate(
        [np.concatenate([cos_t, -sin_t], 2), np.concatenate([sin_t, cos_t], 2)], 1
    )
    dft = np.stack([dft, dft.transpose(0, 2, 1)])
    fwd_hl = np.stack(halves(fwd))
    inv_hl = np.stack(halves(inv))
    dft_hl = np.stack(halves(dft), 1)
    return fwd_hl, inv_hl, dft_hl, twiddle, middle


def split(value):
    high = value.astype(BF16)
    return high, (value - high.astype(F32)).astype(BF16)


def mm(left, right):
    return jnp.dot(left, right, preferred_element_type=F32)


def table_dot(table_ref, value):
    high, low = split(value)
    return mm(table_ref[0], high) + mm(table_ref[0], low) + mm(table_ref[1], high)


def radix4(parts, direction):
    (ar, ai), (br, bi), (cr, ci), (dr, di) = parts
    pr, pi, qr, qi = ar + cr, ai + ci, ar - cr, ai - ci
    sr, si, tr, ti = br + dr, bi + di, br - dr, bi - di
    plus = (qr - ti, qi + tr)
    minus = (qr + ti, qi - tr)
    if direction < 0:
        plus, minus = minus, plus
    return (pr + sr, pi + si), plus, (pr - sr, pi - si), minus


def offsets(shape):
    every = [o for o in itertools.product(*[range(n) for n in shape]) if any(o)]
    random.Random(1).shuffle(every)

    def hops(o):
        z, _, x, y = [min(d, n - d) for d, n in zip(o, shape)]
        return z + x + y

    every.sort(key=lambda o: -hops(o))
    levels = [[], [], []]
    for o in every:
        z, _, x, y = [int(d > 0) for d in o]
        levels[max(z + x + y, 1) - 1].append(o)
    return levels, every


def kernel(
    shape,
    signal_hbm,
    spectrum_hbm,
    dft_hbm,
    fwd_hbm,
    inv_hbm,
    twiddle_hbm,
    middle_hbm,
    gain_hbm,
    out_ref,
    signal,
    spectrum,
    dft,
    fwd,
    inv,
    twiddle,
    middle,
    gain,
    send_x,
    recv_x,
    send_f,
    recv_f,
    send_y,
    recv_y,
    parts,
    bins,
    back,
    load_sem,
    x_sem,
    f_sem,
    y_sem,
    second_sem,
    third_sem,
):
    n_z, n_core, n_x, n_y = shape
    outer = lax.axis_index("outer")
    inner = lax.axis_index("inner")
    n_outer = n_z * n_core
    n_inner = n_x * n_y
    blocks = n_outer * n_inner
    me = outer * n_inner + inner
    slots = blocks // 2
    seq_len = signal.shape[0]
    m_tiles = seq_len // LANES
    rows = 2 * m_tiles
    lines = bins.shape[2]

    def lanes(tile):
        return pl.ds(tile * LANES, LANES)

    z, core = outer // n_core, lax.rem(outer, n_core)
    x, y = inner // n_y, lax.rem(inner, n_y)
    at_outer = [
        [lax.rem(z + d, n_z) * n_core + lax.rem(core + e, n_core) for e in range(n_core)]
        for d in range(n_z)
    ]
    at_x = [lax.rem(x + d, n_x) * n_y for d in range(n_x)]
    at_y = [lax.rem(y + d, n_y) for d in range(n_y)]
    levels, far = offsets(shape)

    def device(offset):
        dz, dc, dx, dy = offset
        return at_outer[dz][dc], at_x[dx] + at_y[dy]

    def tell(sem):
        for offset in levels[0]:
            pl.semaphore_signal(
                sem,
                inc=1,
                device_id=device(offset),
                device_id_type=pl.DeviceIdType.MESH,
            )

    def hear(sem):
        pl.semaphore_wait(sem, len(levels[0]))

    barrier = pltpu.get_barrier_semaphore()
    tell(barrier)

    loads = {}

    def load(name, src, dst):
        copy = pltpu.make_async_copy(src, dst, load_sem.at[len(loads)])
        copy.start()
        loads[name] = copy

    for g in range(2):
        for h in range(2):
            where = lanes(2 * h + g)
            load(("x", g, h), signal_hbm.at[:, where], signal.at[:, where])
        load(("f", g), spectrum_hbm.at[:, :, lanes(g)], spectrum.at[g])
    load("fwd", fwd_hbm, fwd)
    load("twiddle", twiddle_hbm, twiddle)
    load("middle", middle_hbm, middle)
    load("dft", dft_hbm, dft)
    load("inv", inv_hbm, inv)
    load("gain", gain_hbm, gain)

    def block(ref, index):
        return ref.at[pl.ds(pl.multiple_of(index * rows, rows), rows)]

    def send(src, dst, sems, order):
        for offset in order:
            to = device(offset)
            pltpu.make_async_remote_copy(
                src_ref=block(src, to[0] * n_inner + to[1]),
                dst_ref=block(dst, me),
                send_sem=sems.at[0],
                recv_sem=sems.at[1],
                device_id=to,
                device_id_type=pl.DeviceIdType.MESH,
            ).start()

    def keep(src, dst):
        own = pl.ds(pl.multiple_of(me * rows, rows), rows)
        dst[own, :] = src[own, :]

    def wait_all(ref, sem):
        part = ref.at[pl.ds(0, (blocks - 1) * rows)]
        pltpu.make_async_copy(part, part, sem).wait()

    def spread(ref, g, index, tile):
        ref[g, pl.ds(index, blocks, stride=rows), :] = tile

    def send_signal(g, order):
        send(send_x.at[g], recv_x.at[g], x_sem.at[g], order)

    def send_filter(g, order):
        send(send_f.at[g], recv_f.at[g], f_sem.at[g], order)

    for g in range(2):
        for h in range(2):
            loads["x", g, h].wait()
            for mt in range(m_tiles):
                spread(send_x, g, h * m_tiles + mt, signal[lanes(mt), lanes(2 * h + g)].T)
        if g == 0:
            hear(barrier)
            tell(second_sem)
        send_signal(g, levels[0])
        loads["f", g].wait()
        for r in range(2):
            for q in range(RADIX):
                every = pl.ds(q, LANES, stride=RADIX)
                spread(send_f, g, r * m_tiles + q, spectrum[g, r, every, :].T)
        send_filter(g, levels[0])
    hear(second_sem)
    tell(third_sem)
    send_signal(0, levels[1])
    send_filter(0, levels[1])
    hear(third_sem)
    send_signal(0, levels[2])
    send_filter(0, levels[2])
    later = [o for o in far if o not in levels[0]]
    send_signal(1, later)
    send_filter(1, later)
    for g in range(2):
        keep(send_x.at[g], recv_x.at[g])
        keep(send_f.at[g], recv_f.at[g])

    for name in ("fwd", "twiddle", "middle", "dft", "inv", "gain"):
        loads[name].wait()
    first = lax.broadcasted_iota(jnp.int32, (slots, LANES), 0) == 0
    lane = lax.broadcasted_iota(jnp.int32, (1, LANES), 1)
    extra_rows = lines - 2 * slots
    pad = jnp.zeros((extra_rows - 2, LANES), F32)
    tiles = [slice(p * LANES, (p + 1) * LANES) for p in range(RADIX)]

    def put(p, at, count, re, im):
        value = jnp.concatenate([re, im], 1)
        high, low = split(value)
        parts[p, pl.ds(at, count), :] = high
        parts[p, pl.ds(lines + at, count), :] = low

    def transform(p, way):
        whole = mm(parts[p], dft[way, 0, p])
        rest = mm(parts[p, :lines], dft[way, 1, p])
        return whole[:lines] + whole[lines:] + rest

    def forward(g):
        extra = []

        def lines_in(at, count, pairs):
            for p, (re, im) in enumerate(radix4(pairs, -1)):
                put(p, at, count, re, im)

        for h in range(2):
            data = jnp.concatenate(
                [
                    recv_x[g, pl.ds(h * m_tiles + mt, blocks, stride=rows), :]
                    for mt in range(m_tiles)
                ],
                1,
            )
            packed = table_dot(fwd, data)
            extra.append(packed[slots : slots + 1])
            pairs = []
            for t in tiles:
                re = packed[:slots, t]
                im = packed[slots:, t]
                cos_t = twiddle[0, :, t]
                sin_t = twiddle[1, :, t]
                pairs.append(
                    (
                        re * cos_t + im * sin_t,
                        jnp.where(first, 0.0, im * cos_t - re * sin_t),
                    )
                )
            lines_in(h * slots, slots, pairs)
        pairs = []
        for t in tiles:
            value = jnp.concatenate([extra[0][:, t], extra[1][:, t], pad], 0)
            pairs.append((value * middle[0:1, t], -value * middle[1:2, t]))
        lines_in(2 * slots, extra_rows, pairs)
        for p in range(RADIX):
            bins[g, p] = transform(p, 0)

    def times_filter(g, p, at, count, f_re, f_im):
        x_re = bins[g, p, pl.ds(at, count), :LANES]
        x_im = bins[g, p, pl.ds(at, count), LANES:]
        put(p, at, count, f_re * x_re - f_im * x_im, f_re * x_im + f_im * x_re)

    def backward(g):
        lower = lane < LANES // 2
        for p in range(RADIX):
            mid = []
            for h in range(2):
                f_re, f_im = [
                    recv_f[
                        g, pl.ds((h * 2 + r) * m_tiles + p, slots, stride=2 * rows), :
                    ]
                    for r in range(2)
                ]
                top_re = f_re[0:8]
                top_im = f_im[0:8]
                far_re = pltpu.roll(top_re, LANES // 2, 1)[0:1]
                far_im = pltpu.roll(top_im, LANES // 2, 1)[0:1]
                top_re = top_re[0:1]
                top_im = top_im[0:1]
                mid.append(
                    (
                        jnp.where(lower, 2.0 * far_re, 0.0),
                        jnp.where(lower, 2.0 * far_im, 0.0),
                    )
                )
                base_re = jnp.where(lower, 2.0 * top_re, 0.0)
                base_im = jnp.where(lower, 2.0 * top_im, 0.0)
                if p == 0:
                    base_re = jnp.where(lane == 0, top_re, base_re)
                    base_re = jnp.where(lane == LANES // 2, far_im, base_re)
                    base_im = jnp.where(lane == 0, 0.0, base_im)
                times_filter(
                    g,
                    p,
                    h * slots,
                    slots,
                    jnp.where(first, base_re, f_re),
                    jnp.where(first, base_im, f_im),
                )
            times_filter(
                g,
                p,
                2 * slots,
                extra_rows,
                jnp.concatenate([mid[0][0], mid[1][0], pad], 0),
                jnp.concatenate([mid[0][1], mid[1][1], pad], 0),
            )
        for p in range(RADIX):
            back[p] = transform(p, 1)

        def lines_out(at, count):
            at = pl.ds(at, count)
            return radix4([(back[p, at, :LANES], back[p, at, LANES:]) for p in range(RADIX)], 1)

        tail = [
            re * middle[0:1, t] - im * middle[1:2, t]
            for t, (re, im) in zip(tiles, lines_out(2 * slots, extra_rows))
        ]
        for h in range(2):
            v_re = []
            v_im = []
            for t, end, (re, im) in zip(tiles, tail, lines_out(h * slots, slots)):
                cos_t = twiddle[0, :, t]
                sin_t = twiddle[1, :, t]
                v_re.append(re * cos_t - im * sin_t)
                v_im.append(jnp.where(first, end[h : h + 1], re * sin_t + im * cos_t))
            value = jnp.concatenate(
                [jnp.concatenate(v_re, 1), jnp.concatenate(v_im, 1)], 0
            )
            conv = table_dot(inv, value)
            for mt in range(m_tiles):
                spread(send_y, g, h * m_tiles + mt, conv[:, tiles[mt]])

    for g in range(2):
        wait_all(recv_x.at[g], x_sem.at[g, 1])
        forward(g)
        wait_all(recv_f.at[g], f_sem.at[g, 1])
        backward(g)
        send(send_y.at[g], recv_y.at[g], y_sem.at[g], far)
        keep(send_y.at[g], recv_y.at[g])

    for g in range(2):
        wait_all(send_x.at[g], x_sem.at[g, 0])
        wait_all(send_f.at[g], f_sem.at[g, 0])
        wait_all(send_y.at[g], y_sem.at[g, 0])

    for g in range(2):
        wait_all(recv_y.at[g], y_sem.at[g, 1])
        for h in range(2):
            for mt in range(m_tiles):
                tile = recv_y[g, pl.ds(h * m_tiles + mt, blocks, stride=rows), :]
                at = lanes(2 * h + g)
                out_ref[lanes(mt), at] = tile.T + gain[0:1, at] * signal[lanes(mt), at]


def body(signal, spectrum, skip_gain):
    n_outer = lax.axis_size("outer")
    n_inner = lax.axis_size("inner")
    blocks = n_outer * n_inner
    side = math.isqrt(n_inner)
    shape = (n_outer // 2, 2, side, side)
    seq_len, channels = signal.shape
    fwd, inv, dft, twiddle, middle = tables(blocks, seq_len)
    rows = 2 * (seq_len // LANES)
    lines = blocks + 16
    vmem = pltpu.VMEM
    dma = pltpu.SemaphoreType.DMA
    in_hbm = pl.BlockSpec(memory_space=pltpu.HBM)
    return pl.pallas_call(
        functools.partial(kernel, shape),
        out_shape=jax.ShapeDtypeStruct(signal.shape, F32),
        in_specs=[in_hbm] * 8,
        out_specs=pl.BlockSpec(memory_space=pltpu.VMEM),
        scratch_shapes=[
            vmem(signal.shape, F32),
            vmem((2, 2, seq_len, LANES), F32),
            vmem(dft.shape, BF16),
            vmem(fwd.shape, BF16),
            vmem(inv.shape, BF16),
            vmem(twiddle.shape, F32),
            vmem(middle.shape, F32),
            vmem((1, channels), F32),
            *[vmem((2, blocks * rows, LANES), F32) for _ in range(6)],
            vmem((RADIX, 2 * lines, 2 * LANES), BF16),
            vmem((2, RADIX, lines, 2 * LANES), F32),
            vmem((RADIX, lines, 2 * LANES), F32),
            dma((12,)),
            *[dma((2, 2)) for _ in range(3)],
            pltpu.SemaphoreType.REGULAR,
            pltpu.SemaphoreType.REGULAR,
        ],
        compiler_params=pltpu.CompilerParams(
            collective_id=1, has_side_effects=True, vmem_limit_bytes=48 * 2**20
        ),
        cost_estimate=pl.CostEstimate(
            flops=2 * 10**9, bytes_accessed=8 * 2**20, transcendentals=0
        ),
        name="hyena_conv",
    )(
        *[
            pltpu.with_memory_space_constraint(a, pltpu.HBM)
            for a in (
                signal,
                spectrum.reshape(spectrum.shape[1:]),
                dft,
                fwd,
                inv,
                twiddle,
                middle,
                skip_gain[None, :],
            )
        ]
    )


def solution(mesh):
    return jax.shard_map(
        body,
        mesh=mesh,
        in_specs=(P(("outer", "inner"), None), P(("outer", "inner"), None, None, None), P()),
        out_specs=P(("outer", "inner"), None),
        check_vma=False,
    )
```

```python
import functools
import itertools
import math
import random

import jax
import jax.numpy as jnp
import ml_dtypes
import numpy as np
from jax import lax
from jax.experimental import pallas as pl
from jax.experimental.pallas import tpu as pltpu
from jax.sharding import PartitionSpec as P

F32 = jnp.float32
BF16 = jnp.bfloat16
LANES = 128
RADIX = 4


def halves(table):
    high = table.astype(ml_dtypes.bfloat16)
    low = (table - high.astype(np.float64)).astype(ml_dtypes.bfloat16)
    return high, low


def tables(blocks, seq_len):
    slots = blocks // 2
    total = blocks * seq_len
    d = np.arange(blocks)
    s = np.arange(slots)
    m = np.arange(seq_len)
    angle = 2.0 * math.pi / blocks * (s[:, None] * d[None, :] % blocks)
    cos_rows = np.cos(angle)
    sin_rows = np.sin(angle)
    sin_rows[0] = np.where(d % 2 == 0, -1.0, 1.0)
    fwd = np.concatenate([cos_rows, -sin_rows], 0)
    scale = np.where(s == 0, 1.0, 2.0)[:, None] / total
    inv = (fwd * np.concatenate([scale, scale], 0)).T
    turn = 2.0 * math.pi / total * (np.arange(slots + 1)[:, None] * m[None, :] % total)
    twiddle = np.stack([np.cos(turn[:slots]), np.sin(turn[:slots])]).astype(np.float32)
    middle = np.stack([np.cos(turn[slots]), np.sin(turn[slots])]).astype(np.float32)
    middle = np.concatenate([middle, np.zeros((6, seq_len), np.float32)], 0)
    n = np.arange(LANES)[None, :, None]
    l = np.arange(LANES)[None, None, :]
    r = np.arange(RADIX)[:, None, None]
    theta = 2.0 * math.pi / seq_len * (n * (r + RADIX * l) % seq_len)
    cos_t = np.cos(theta)
    sin_t = np.sin(theta)
    dft = np.concatenate(
        [np.concatenate([cos_t, -sin_t], 2), np.concatenate([sin_t, cos_t], 2)], 1
    )
    dft = np.stack([dft, dft.transpose(0, 2, 1)])
    fwd_hl = np.stack(halves(fwd))
    inv_hl = np.stack(halves(inv))
    dft_hl = np.stack(halves(dft), 1)
    return fwd_hl, inv_hl, dft_hl, twiddle, middle


def split(value):
    high = value.astype(BF16)
    return high, (value - high.astype(F32)).astype(BF16)


def mm(left, right):
    return jnp.dot(left, right, preferred_element_type=F32)


def table_dot(table_ref, value):
    high, low = split(value)
    return mm(table_ref[0], high) + mm(table_ref[0], low) + mm(table_ref[1], high)


def radix4(parts, direction):
    (ar, ai), (br, bi), (cr, ci), (dr, di) = parts
    pr, pi, qr, qi = ar + cr, ai + ci, ar - cr, ai - ci
    sr, si, tr, ti = br + dr, bi + di, br - dr, bi - di
    plus = (qr - ti, qi + tr)
    minus = (qr + ti, qi - tr)
    if direction < 0:
        plus, minus = minus, plus
    return (pr + sr, pi + si), plus, (pr - sr, pi - si), minus


def offsets(shape):
    every = [o for o in itertools.product(*[range(n) for n in shape]) if any(o)]
    random.Random(1).shuffle(every)

    def hops(o):
        z, _, x, y = [min(d, n - d) for d, n in zip(o, shape)]
        return z + x + y

    levels = [[], [], []]
    for o in every:
        z, _, x, y = [int(d > 0) for d in o]
        levels[max(z + x + y, 1) - 1].append(o)
    mixed = list(every)
    every.sort(key=lambda o: -hops(o))
    return levels, every, mixed


def kernel(
    shape,
    signal_hbm,
    spectrum_hbm,
    dft_hbm,
    fwd_hbm,
    inv_hbm,
    twiddle_hbm,
    middle_hbm,
    gain_hbm,
    out_ref,
    signal,
    spectrum,
    dft,
    fwd,
    inv,
    twiddle,
    middle,
    gain,
    send_x,
    recv_x,
    send_f,
    recv_f,
    send_y,
    recv_y,
    parts,
    bins,
    back,
    load_sem,
    x_sem,
    f_sem,
    y_sem,
    second_sem,
    third_sem,
):
    n_z, n_core, n_x, n_y = shape
    outer = lax.axis_index("outer")
    inner = lax.axis_index("inner")
    n_outer = n_z * n_core
    n_inner = n_x * n_y
    blocks = n_outer * n_inner
    me = outer * n_inner + inner
    slots = blocks // 2
    seq_len = signal.shape[0]
    m_tiles = seq_len // LANES
    rows = 2 * m_tiles
    lines = bins.shape[2]

    def lanes(tile):
        return pl.ds(tile * LANES, LANES)

    z, core = outer // n_core, lax.rem(outer, n_core)
    x, y = inner // n_y, lax.rem(inner, n_y)
    at_outer = [
        [lax.rem(z + d, n_z) * n_core + lax.rem(core + e, n_core) for e in range(n_core)]
        for d in range(n_z)
    ]
    at_x = [lax.rem(x + d, n_x) * n_y for d in range(n_x)]
    at_y = [lax.rem(y + d, n_y) for d in range(n_y)]
    levels, far, mixed = offsets(shape)

    def device(offset):
        dz, dc, dx, dy = offset
        return at_outer[dz][dc], at_x[dx] + at_y[dy]

    def tell(sem):
        for offset in levels[0]:
            pl.semaphore_signal(
                sem,
                inc=1,
                device_id=device(offset),
                device_id_type=pl.DeviceIdType.MESH,
            )

    def hear(sem):
        pl.semaphore_wait(sem, len(levels[0]))

    barrier = pltpu.get_barrier_semaphore()
    tell(barrier)

    loads = {}

    def load(name, src, dst):
        copy = pltpu.make_async_copy(src, dst, load_sem.at[len(loads)])
        copy.start()
        loads[name] = copy

    for g in range(2):
        for h in range(2):
            where = lanes(2 * h + g)
            load(("x", g, h), signal_hbm.at[:, where], signal.at[:, where])
        load(("f", g), spectrum_hbm.at[:, :, lanes(g)], spectrum.at[g])
    load("fwd", fwd_hbm, fwd)
    load("twiddle", twiddle_hbm, twiddle)
    load("middle", middle_hbm, middle)
    load("dft", dft_hbm, dft)
    load("inv", inv_hbm, inv)
    load("gain", gain_hbm, gain)

    def block(ref, index):
        return ref.at[pl.ds(pl.multiple_of(index * rows, rows), rows)]

    def send(src, dst, sems, order):
        for offset in order:
            to = device(offset)
            pltpu.make_async_remote_copy(
                src_ref=block(src, to[0] * n_inner + to[1]),
                dst_ref=block(dst, me),
                send_sem=sems.at[0],
                recv_sem=sems.at[1],
                device_id=to,
                device_id_type=pl.DeviceIdType.MESH,
            ).start()

    def keep(src, dst):
        own = pl.ds(pl.multiple_of(me * rows, rows), rows)
        dst[own, :] = src[own, :]

    def wait_all(ref, sem):
        part = ref.at[pl.ds(0, (blocks - 1) * rows)]
        pltpu.make_async_copy(part, part, sem).wait()

    def spread(ref, g, index, tile):
        ref[g, pl.ds(index, blocks, stride=rows), :] = tile

    def send_signal(g, order):
        send(send_x.at[g], recv_x.at[g], x_sem.at[g], order)

    def send_filter(g, order):
        send(send_f.at[g], recv_f.at[g], f_sem.at[g], order)

    for g in range(2):
        for h in range(2):
            loads["x", g, h].wait()
            for mt in range(m_tiles):
                spread(send_x, g, h * m_tiles + mt, signal[lanes(mt), lanes(2 * h + g)].T)
        if g == 0:
            hear(barrier)
            tell(second_sem)
        send_signal(g, levels[0])
        loads["f", g].wait()
        for r in range(2):
            for q in range(RADIX):
                every = pl.ds(q, LANES, stride=RADIX)
                spread(send_f, g, r * m_tiles + q, spectrum[g, r, every, :].T)
        send_filter(g, levels[0])
    hear(second_sem)
    tell(third_sem)
    send_signal(0, levels[1])
    send_filter(0, levels[1])
    hear(third_sem)
    send_signal(0, levels[2])
    send_filter(0, levels[2])
    later = [o for o in far if o not in levels[0]]
    send_signal(1, [o for o in mixed if o not in levels[0]])
    send_filter(1, later)
    for g in range(2):
        keep(send_x.at[g], recv_x.at[g])
        keep(send_f.at[g], recv_f.at[g])

    for name in ("fwd", "twiddle", "middle", "dft", "inv", "gain"):
        loads[name].wait()
    first = lax.broadcasted_iota(jnp.int32, (slots, LANES), 0) == 0
    lane = lax.broadcasted_iota(jnp.int32, (1, LANES), 1)
    extra_rows = lines - 2 * slots
    pad = jnp.zeros((extra_rows - 2, LANES), F32)
    tiles = [slice(p * LANES, (p + 1) * LANES) for p in range(RADIX)]

    def put(p, at, count, re, im):
        value = jnp.concatenate([re, im], 1)
        high, low = split(value)
        parts[p, pl.ds(at, count), :] = high
        parts[p, pl.ds(lines + at, count), :] = low

    def transform(p, way):
        whole = mm(parts[p], dft[way, 0, p])
        rest = mm(parts[p, :lines], dft[way, 1, p])
        return whole[:lines] + whole[lines:] + rest

    def forward(g):
        extra = []

        def lines_in(at, count, pairs):
            for p, (re, im) in enumerate(radix4(pairs, -1)):
                put(p, at, count, re, im)

        for h in range(2):
            data = jnp.concatenate(
                [
                    recv_x[g, pl.ds(h * m_tiles + mt, blocks, stride=rows), :]
                    for mt in range(m_tiles)
                ],
                1,
            )
            packed = table_dot(fwd, data)
            extra.append(packed[slots : slots + 1])
            pairs = []
            for t in tiles:
                re = packed[:slots, t]
                im = packed[slots:, t]
                cos_t = twiddle[0, :, t]
                sin_t = twiddle[1, :, t]
                pairs.append(
                    (
                        re * cos_t + im * sin_t,
                        jnp.where(first, 0.0, im * cos_t - re * sin_t),
                    )
                )
            lines_in(h * slots, slots, pairs)
        pairs = []
        for t in tiles:
            value = jnp.concatenate([extra[0][:, t], extra[1][:, t], pad], 0)
            pairs.append((value * middle[0:1, t], -value * middle[1:2, t]))
        lines_in(2 * slots, extra_rows, pairs)
        for p in range(RADIX):
            bins[g, p] = transform(p, 0)

    def times_filter(g, p, at, count, f_re, f_im):
        x_re = bins[g, p, pl.ds(at, count), :LANES]
        x_im = bins[g, p, pl.ds(at, count), LANES:]
        put(p, at, count, f_re * x_re - f_im * x_im, f_re * x_im + f_im * x_re)

    def backward(g):
        lower = lane < LANES // 2
        for p in range(RADIX):
            mid = []
            for h in range(2):
                f_re, f_im = [
                    recv_f[
                        g, pl.ds((h * 2 + r) * m_tiles + p, slots, stride=2 * rows), :
                    ]
                    for r in range(2)
                ]
                top_re = f_re[0:8]
                top_im = f_im[0:8]
                far_re = pltpu.roll(top_re, LANES // 2, 1)[0:1]
                far_im = pltpu.roll(top_im, LANES // 2, 1)[0:1]
                top_re = top_re[0:1]
                top_im = top_im[0:1]
                mid.append(
                    (
                        jnp.where(lower, 2.0 * far_re, 0.0),
                        jnp.where(lower, 2.0 * far_im, 0.0),
                    )
                )
                base_re = jnp.where(lower, 2.0 * top_re, 0.0)
                base_im = jnp.where(lower, 2.0 * top_im, 0.0)
                if p == 0:
                    base_re = jnp.where(lane == 0, top_re, base_re)
                    base_re = jnp.where(lane == LANES // 2, far_im, base_re)
                    base_im = jnp.where(lane == 0, 0.0, base_im)
                times_filter(
                    g,
                    p,
                    h * slots,
                    slots,
                    jnp.where(first, base_re, f_re),
                    jnp.where(first, base_im, f_im),
                )
            times_filter(
                g,
                p,
                2 * slots,
                extra_rows,
                jnp.concatenate([mid[0][0], mid[1][0], pad], 0),
                jnp.concatenate([mid[0][1], mid[1][1], pad], 0),
            )
        for p in range(RADIX):
            back[p] = transform(p, 1)

        def lines_out(at, count):
            at = pl.ds(at, count)
            return radix4([(back[p, at, :LANES], back[p, at, LANES:]) for p in range(RADIX)], 1)

        tail = [
            re * middle[0:1, t] - im * middle[1:2, t]
            for t, (re, im) in zip(tiles, lines_out(2 * slots, extra_rows))
        ]
        for h in range(2):
            v_re = []
            v_im = []
            for t, end, (re, im) in zip(tiles, tail, lines_out(h * slots, slots)):
                cos_t = twiddle[0, :, t]
                sin_t = twiddle[1, :, t]
                v_re.append(re * cos_t - im * sin_t)
                v_im.append(jnp.where(first, end[h : h + 1], re * sin_t + im * cos_t))
            value = jnp.concatenate(
                [jnp.concatenate(v_re, 1), jnp.concatenate(v_im, 1)], 0
            )
            conv = table_dot(inv, value)
            for mt in range(m_tiles):
                spread(send_y, g, h * m_tiles + mt, conv[:, tiles[mt]])

    for g in range(2):
        wait_all(recv_x.at[g], x_sem.at[g, 1])
        forward(g)
        wait_all(recv_f.at[g], f_sem.at[g, 1])
        backward(g)
        send(send_y.at[g], recv_y.at[g], y_sem.at[g], (mixed, far)[g])
        keep(send_y.at[g], recv_y.at[g])

    for g in range(2):
        wait_all(send_x.at[g], x_sem.at[g, 0])
        wait_all(send_f.at[g], f_sem.at[g, 0])
        wait_all(send_y.at[g], y_sem.at[g, 0])

    for g in range(2):
        wait_all(recv_y.at[g], y_sem.at[g, 1])
        for h in range(2):
            for mt in range(m_tiles):
                tile = recv_y[g, pl.ds(h * m_tiles + mt, blocks, stride=rows), :]
                at = lanes(2 * h + g)
                out_ref[lanes(mt), at] = tile.T + gain[0:1, at] * signal[lanes(mt), at]


def body(signal, spectrum, skip_gain):
    n_outer = lax.axis_size("outer")
    n_inner = lax.axis_size("inner")
    blocks = n_outer * n_inner
    side = math.isqrt(n_inner)
    shape = (n_outer // 2, 2, side, side)
    seq_len, channels = signal.shape
    fwd, inv, dft, twiddle, middle = tables(blocks, seq_len)
    rows = 2 * (seq_len // LANES)
    lines = blocks + 16
    vmem = pltpu.VMEM
    dma = pltpu.SemaphoreType.DMA
    in_hbm = pl.BlockSpec(memory_space=pltpu.HBM)
    return pl.pallas_call(
        functools.partial(kernel, shape),
        out_shape=jax.ShapeDtypeStruct(signal.shape, F32),
        in_specs=[in_hbm] * 8,
        out_specs=pl.BlockSpec(memory_space=pltpu.VMEM),
        scratch_shapes=[
            vmem(signal.shape, F32),
            vmem((2, 2, seq_len, LANES), F32),
            vmem(dft.shape, BF16),
            vmem(fwd.shape, BF16),
            vmem(inv.shape, BF16),
            vmem(twiddle.shape, F32),
            vmem(middle.shape, F32),
            vmem((1, channels), F32),
            *[vmem((2, blocks * rows, LANES), F32) for _ in range(6)],
            vmem((RADIX, 2 * lines, 2 * LANES), BF16),
            vmem((2, RADIX, lines, 2 * LANES), F32),
            vmem((RADIX, lines, 2 * LANES), F32),
            dma((12,)),
            *[dma((2, 2)) for _ in range(3)],
            pltpu.SemaphoreType.REGULAR,
            pltpu.SemaphoreType.REGULAR,
        ],
        compiler_params=pltpu.CompilerParams(
            collective_id=1, has_side_effects=True, vmem_limit_bytes=48 * 2**20
        ),
        cost_estimate=pl.CostEstimate(
            flops=2 * 10**9, bytes_accessed=8 * 2**20, transcendentals=0
        ),
        name="hyena_conv",
    )(
        *[
            pltpu.with_memory_space_constraint(a, pltpu.HBM)
            for a in (
                signal,
                spectrum.reshape(spectrum.shape[1:]),
                dft,
                fwd,
                inv,
                twiddle,
                middle,
                skip_gain[None, :],
            )
        ]
    )


def solution(mesh):
    return jax.shard_map(
        body,
        mesh=mesh,
        in_specs=(P(("outer", "inner"), None), P(("outer", "inner"), None, None, None), P()),
        out_specs=P(("outer", "inner"), None),
        check_vma=False,
    )
```

```python
import functools
import itertools
import math
import random

import jax
import jax.numpy as jnp
import ml_dtypes
import numpy as np
from jax import lax
from jax.experimental import pallas as pl
from jax.experimental.pallas import tpu as pltpu
from jax.sharding import PartitionSpec as P

F32 = jnp.float32
BF16 = jnp.bfloat16
LANES = 128
RADIX = 4


def halves(table):
    high = table.astype(ml_dtypes.bfloat16)
    low = (table - high.astype(np.float64)).astype(ml_dtypes.bfloat16)
    return high, low


def tables(blocks, seq_len):
    slots = blocks // 2
    total = blocks * seq_len
    d = np.arange(blocks)
    s = np.arange(slots)
    m = np.arange(seq_len)
    angle = 2.0 * math.pi / blocks * (s[:, None] * d[None, :] % blocks)
    cos_rows = np.cos(angle)
    sin_rows = np.sin(angle)
    sin_rows[0] = np.where(d % 2 == 0, -1.0, 1.0)
    fwd = np.concatenate([cos_rows, -sin_rows], 0)
    scale = np.where(s == 0, 1.0, 2.0)[:, None] / total
    inv = (fwd * np.concatenate([scale, scale], 0)).T
    turn = 2.0 * math.pi / total * (np.arange(slots + 1)[:, None] * m[None, :] % total)
    twiddle = np.stack([np.cos(turn[:slots]), np.sin(turn[:slots])]).astype(np.float32)
    middle = np.stack([np.cos(turn[slots]), np.sin(turn[slots])]).astype(np.float32)
    middle = np.concatenate([middle, np.zeros((6, seq_len), np.float32)], 0)
    n = np.arange(LANES)[None, :, None]
    l = np.arange(LANES)[None, None, :]
    r = np.arange(RADIX)[:, None, None]
    theta = 2.0 * math.pi / seq_len * (n * (r + RADIX * l) % seq_len)
    cos_t = np.cos(theta)
    sin_t = np.sin(theta)
    dft = np.concatenate(
        [np.concatenate([cos_t, -sin_t], 2), np.concatenate([sin_t, cos_t], 2)], 1
    )
    dft = np.stack([dft, dft.transpose(0, 2, 1)])
    fwd_hl = np.stack(halves(fwd))
    inv_hl = np.stack(halves(inv))
    dft_hl = np.stack(halves(dft), 1)
    return fwd_hl, inv_hl, dft_hl, twiddle, middle


def split(value):
    high = value.astype(BF16)
    return high, (value - high.astype(F32)).astype(BF16)


def mm(left, right):
    return jnp.dot(left, right, preferred_element_type=F32)


def table_dot(table_ref, value):
    high, low = split(value)
    return mm(table_ref[0], high) + mm(table_ref[0], low) + mm(table_ref[1], high)


def radix4(parts, direction):
    (ar, ai), (br, bi), (cr, ci), (dr, di) = parts
    pr, pi, qr, qi = ar + cr, ai + ci, ar - cr, ai - ci
    sr, si, tr, ti = br + dr, bi + di, br - dr, bi - di
    plus = (qr - ti, qi + tr)
    minus = (qr + ti, qi - tr)
    if direction < 0:
        plus, minus = minus, plus
    return (pr + sr, pi + si), plus, (pr - sr, pi - si), minus


def offsets(shape):
    every = [o for o in itertools.product(*[range(n) for n in shape]) if any(o)]
    random.Random(1).shuffle(every)

    def hops(o):
        z, _, x, y = [min(d, n - d) for d, n in zip(o, shape)]
        return z + x + y

    levels = [[], [], []]
    for o in every:
        z, _, x, y = [int(d > 0) for d in o]
        levels[max(z + x + y, 1) - 1].append(o)
    mixed = list(every)
    every.sort(key=lambda o: -hops(o))
    return levels, every, mixed


def kernel(
    shape,
    signal_hbm,
    spectrum_hbm,
    dft_hbm,
    fwd_hbm,
    inv_hbm,
    twiddle_hbm,
    middle_hbm,
    gain_hbm,
    out_ref,
    signal,
    spectrum,
    dft,
    fwd,
    inv,
    twiddle,
    middle,
    gain,
    send_x,
    recv_x,
    send_f,
    recv_f,
    send_y,
    recv_y,
    parts,
    bins,
    back,
    load_sem,
    x_sem,
    f_sem,
    y_sem,
    second_sem,
    third_sem,
):
    n_z, n_core, n_x, n_y = shape
    outer = lax.axis_index("outer")
    inner = lax.axis_index("inner")
    n_outer = n_z * n_core
    n_inner = n_x * n_y
    blocks = n_outer * n_inner
    me = outer * n_inner + inner
    slots = blocks // 2
    seq_len = signal.shape[0]
    m_tiles = seq_len // LANES
    rows = 2 * m_tiles
    lines = bins.shape[2]

    def lanes(tile):
        return pl.ds(tile * LANES, LANES)

    z, core = outer // n_core, lax.rem(outer, n_core)
    x, y = inner // n_y, lax.rem(inner, n_y)
    at_outer = [
        [lax.rem(z + d, n_z) * n_core + lax.rem(core + e, n_core) for e in range(n_core)]
        for d in range(n_z)
    ]
    at_x = [lax.rem(x + d, n_x) * n_y for d in range(n_x)]
    at_y = [lax.rem(y + d, n_y) for d in range(n_y)]
    levels, far, mixed = offsets(shape)

    def device(offset):
        dz, dc, dx, dy = offset
        return at_outer[dz][dc], at_x[dx] + at_y[dy]

    def tell(sem):
        for offset in levels[0]:
            pl.semaphore_signal(
                sem,
                inc=1,
                device_id=device(offset),
                device_id_type=pl.DeviceIdType.MESH,
            )

    def hear(sem):
        pl.semaphore_wait(sem, len(levels[0]))

    barrier = pltpu.get_barrier_semaphore()
    tell(barrier)

    loads = {}

    def load(name, src, dst):
        copy = pltpu.make_async_copy(src, dst, load_sem.at[len(loads)])
        copy.start()
        loads[name] = copy

    for g in range(2):
        for h in range(2):
            where = lanes(2 * h + g)
            load(("x", g, h), signal_hbm.at[:, where], signal.at[:, where])
        load(("f", g), spectrum_hbm.at[:, :, lanes(g)], spectrum.at[g])
    load("fwd", fwd_hbm, fwd)
    load("twiddle", twiddle_hbm, twiddle)
    load("middle", middle_hbm, middle)
    load("dft", dft_hbm, dft)
    load("inv", inv_hbm, inv)
    load("gain", gain_hbm, gain)

    def block(ref, index):
        return ref.at[pl.ds(pl.multiple_of(index * rows, rows), rows)]

    def send_one(src, dst, sems, to):
        pltpu.make_async_remote_copy(
            src_ref=block(src, to[0] * n_inner + to[1]),
            dst_ref=block(dst, me),
            send_sem=sems.at[0],
            recv_sem=sems.at[1],
            device_id=to,
            device_id_type=pl.DeviceIdType.MESH,
        ).start()

    def send(src, dst, sems, order):
        for offset in order:
            send_one(src, dst, sems, device(offset))

    def hops(d, n):
        return jnp.minimum(d, n - d)

    def send_last(src, dst, sems):
        near = hops(z, n_z) + hops(x, n_x) + hops(y, n_y) <= 2
        for c in range(n_core):

            @pl.when(near & ((outer != c) | (inner != 0)))
            def _():
                send_one(src, dst, sems, (c, 0))

        for offset in far:
            to = device(offset)
            dz, _, dx, dy = offset
            if min(dz, n_z - dz) + min(dx, n_x - dx) + min(dy, n_y - dy) > 2:
                send_one(src, dst, sems, to)
            else:

                @pl.when((to[0] >= n_core) | (to[1] != 0))
                def _():
                    send_one(src, dst, sems, to)

    def keep(src, dst):
        own = pl.ds(pl.multiple_of(me * rows, rows), rows)
        dst[own, :] = src[own, :]

    def wait_all(ref, sem):
        part = ref.at[pl.ds(0, (blocks - 1) * rows)]
        pltpu.make_async_copy(part, part, sem).wait()

    def spread(ref, g, index, tile):
        ref[g, pl.ds(index, blocks, stride=rows), :] = tile

    def send_signal(g, order):
        send(send_x.at[g], recv_x.at[g], x_sem.at[g], order)

    def send_filter(g, order):
        send(send_f.at[g], recv_f.at[g], f_sem.at[g], order)

    for g in range(2):
        for h in range(2):
            loads["x", g, h].wait()
            for mt in range(m_tiles):
                spread(send_x, g, h * m_tiles + mt, signal[lanes(mt), lanes(2 * h + g)].T)
        if g == 0:
            hear(barrier)
            tell(second_sem)
        send_signal(g, levels[0])
        loads["f", g].wait()
        for r in range(2):
            for q in range(RADIX):
                every = pl.ds(q, LANES, stride=RADIX)
                spread(send_f, g, r * m_tiles + q, spectrum[g, r, every, :].T)
        send_filter(g, levels[0])
    hear(second_sem)
    tell(third_sem)
    send_signal(0, levels[1])
    send_filter(0, levels[1])
    hear(third_sem)
    send_signal(0, levels[2])
    send_filter(0, levels[2])
    later = [o for o in far if o not in levels[0]]
    send_signal(1, [o for o in mixed if o not in levels[0]])
    send_filter(1, later)
    for g in range(2):
        keep(send_x.at[g], recv_x.at[g])
        keep(send_f.at[g], recv_f.at[g])

    for name in ("fwd", "twiddle", "middle", "dft", "inv", "gain"):
        loads[name].wait()
    first = lax.broadcasted_iota(jnp.int32, (slots, LANES), 0) == 0
    lane = lax.broadcasted_iota(jnp.int32, (1, LANES), 1)
    extra_rows = lines - 2 * slots
    pad = jnp.zeros((extra_rows - 2, LANES), F32)
    tiles = [slice(p * LANES, (p + 1) * LANES) for p in range(RADIX)]

    def put(p, at, count, re, im):
        value = jnp.concatenate([re, im], 1)
        high, low = split(value)
        parts[p, pl.ds(at, count), :] = high
        parts[p, pl.ds(lines + at, count), :] = low

    def transform(p, way):
        whole = mm(parts[p], dft[way, 0, p])
        rest = mm(parts[p, :lines], dft[way, 1, p])
        return whole[:lines] + whole[lines:] + rest

    def forward(g):
        extra = []

        def lines_in(at, count, pairs):
            for p, (re, im) in enumerate(radix4(pairs, -1)):
                put(p, at, count, re, im)

        for h in range(2):
            data = jnp.concatenate(
                [
                    recv_x[g, pl.ds(h * m_tiles + mt, blocks, stride=rows), :]
                    for mt in range(m_tiles)
                ],
                1,
            )
            packed = table_dot(fwd, data)
            extra.append(packed[slots : slots + 1])
            pairs = []
            for t in tiles:
                re = packed[:slots, t]
                im = packed[slots:, t]
                cos_t = twiddle[0, :, t]
                sin_t = twiddle[1, :, t]
                pairs.append(
                    (
                        re * cos_t + im * sin_t,
                        jnp.where(first, 0.0, im * cos_t - re * sin_t),
                    )
                )
            lines_in(h * slots, slots, pairs)
        pairs = []
        for t in tiles:
            value = jnp.concatenate([extra[0][:, t], extra[1][:, t], pad], 0)
            pairs.append((value * middle[0:1, t], -value * middle[1:2, t]))
        lines_in(2 * slots, extra_rows, pairs)
        for p in range(RADIX):
            bins[g, p] = transform(p, 0)

    def times_filter(g, p, at, count, f_re, f_im):
        x_re = bins[g, p, pl.ds(at, count), :LANES]
        x_im = bins[g, p, pl.ds(at, count), LANES:]
        put(p, at, count, f_re * x_re - f_im * x_im, f_re * x_im + f_im * x_re)

    def backward(g):
        lower = lane < LANES // 2
        for p in range(RADIX):
            mid = []
            for h in range(2):
                f_re, f_im = [
                    recv_f[
                        g, pl.ds((h * 2 + r) * m_tiles + p, slots, stride=2 * rows), :
                    ]
                    for r in range(2)
                ]
                top_re = f_re[0:8]
                top_im = f_im[0:8]
                far_re = pltpu.roll(top_re, LANES // 2, 1)[0:1]
                far_im = pltpu.roll(top_im, LANES // 2, 1)[0:1]
                top_re = top_re[0:1]
                top_im = top_im[0:1]
                mid.append(
                    (
                        jnp.where(lower, 2.0 * far_re, 0.0),
                        jnp.where(lower, 2.0 * far_im, 0.0),
                    )
                )
                base_re = jnp.where(lower, 2.0 * top_re, 0.0)
                base_im = jnp.where(lower, 2.0 * top_im, 0.0)
                if p == 0:
                    base_re = jnp.where(lane == 0, top_re, base_re)
                    base_re = jnp.where(lane == LANES // 2, far_im, base_re)
                    base_im = jnp.where(lane == 0, 0.0, base_im)
                times_filter(
                    g,
                    p,
                    h * slots,
                    slots,
                    jnp.where(first, base_re, f_re),
                    jnp.where(first, base_im, f_im),
                )
            times_filter(
                g,
                p,
                2 * slots,
                extra_rows,
                jnp.concatenate([mid[0][0], mid[1][0], pad], 0),
                jnp.concatenate([mid[0][1], mid[1][1], pad], 0),
            )
        for p in range(RADIX):
            back[p] = transform(p, 1)

        def lines_out(at, count):
            at = pl.ds(at, count)
            return radix4([(back[p, at, :LANES], back[p, at, LANES:]) for p in range(RADIX)], 1)

        tail = [
            re * middle[0:1, t] - im * middle[1:2, t]
            for t, (re, im) in zip(tiles, lines_out(2 * slots, extra_rows))
        ]
        for h in range(2):
            v_re = []
            v_im = []
            for t, end, (re, im) in zip(tiles, tail, lines_out(h * slots, slots)):
                cos_t = twiddle[0, :, t]
                sin_t = twiddle[1, :, t]
                v_re.append(re * cos_t - im * sin_t)
                v_im.append(jnp.where(first, end[h : h + 1], re * sin_t + im * cos_t))
            value = jnp.concatenate(
                [jnp.concatenate(v_re, 1), jnp.concatenate(v_im, 1)], 0
            )
            conv = table_dot(inv, value)
            for mt in range(m_tiles):
                spread(send_y, g, h * m_tiles + mt, conv[:, tiles[mt]])

    for g in range(2):
        wait_all(recv_x.at[g], x_sem.at[g, 1])
        forward(g)
        wait_all(recv_f.at[g], f_sem.at[g, 1])
        backward(g)
        if g == 0:
            send(send_y.at[g], recv_y.at[g], y_sem.at[g], mixed)
        else:
            send_last(send_y.at[g], recv_y.at[g], y_sem.at[g])
        keep(send_y.at[g], recv_y.at[g])

    for g in range(2):
        wait_all(send_x.at[g], x_sem.at[g, 0])
        wait_all(send_f.at[g], f_sem.at[g, 0])
        wait_all(send_y.at[g], y_sem.at[g, 0])

    for g in range(2):
        wait_all(recv_y.at[g], y_sem.at[g, 1])
        for h in range(2):
            for mt in range(m_tiles):
                tile = recv_y[g, pl.ds(h * m_tiles + mt, blocks, stride=rows), :]
                at = lanes(2 * h + g)
                out_ref[lanes(mt), at] = tile.T + gain[0:1, at] * signal[lanes(mt), at]


def body(signal, spectrum, skip_gain):
    n_outer = lax.axis_size("outer")
    n_inner = lax.axis_size("inner")
    blocks = n_outer * n_inner
    side = math.isqrt(n_inner)
    shape = (n_outer // 2, 2, side, side)
    seq_len, channels = signal.shape
    fwd, inv, dft, twiddle, middle = tables(blocks, seq_len)
    rows = 2 * (seq_len // LANES)
    lines = blocks + 16
    vmem = pltpu.VMEM
    dma = pltpu.SemaphoreType.DMA
    in_hbm = pl.BlockSpec(memory_space=pltpu.HBM)
    return pl.pallas_call(
        functools.partial(kernel, shape),
        out_shape=jax.ShapeDtypeStruct(signal.shape, F32),
        in_specs=[in_hbm] * 8,
        out_specs=pl.BlockSpec(memory_space=pltpu.VMEM),
        scratch_shapes=[
            vmem(signal.shape, F32),
            vmem((2, 2, seq_len, LANES), F32),
            vmem(dft.shape, BF16),
            vmem(fwd.shape, BF16),
            vmem(inv.shape, BF16),
            vmem(twiddle.shape, F32),
            vmem(middle.shape, F32),
            vmem((1, channels), F32),
            *[vmem((2, blocks * rows, LANES), F32) for _ in range(6)],
            vmem((RADIX, 2 * lines, 2 * LANES), BF16),
            vmem((2, RADIX, lines, 2 * LANES), F32),
            vmem((RADIX, lines, 2 * LANES), F32),
            dma((12,)),
            *[dma((2, 2)) for _ in range(3)],
            pltpu.SemaphoreType.REGULAR,
            pltpu.SemaphoreType.REGULAR,
        ],
        compiler_params=pltpu.CompilerParams(
            collective_id=1, has_side_effects=True, vmem_limit_bytes=48 * 2**20
        ),
        cost_estimate=pl.CostEstimate(
            flops=2 * 10**9, bytes_accessed=8 * 2**20, transcendentals=0
        ),
        name="hyena_conv",
    )(
        *[
            pltpu.with_memory_space_constraint(a, pltpu.HBM)
            for a in (
                signal,
                spectrum.reshape(spectrum.shape[1:]),
                dft,
                fwd,
                inv,
                twiddle,
                middle,
                skip_gain[None, :],
            )
        ]
    )


def solution(mesh):
    return jax.shard_map(
        body,
        mesh=mesh,
        in_specs=(P(("outer", "inner"), None), P(("outer", "inner"), None, None, None), P()),
        out_specs=P(("outer", "inner"), None),
        check_vma=False,
    )
```

```python
import functools
import itertools
import math
import random

import jax
import jax.numpy as jnp
import ml_dtypes
import numpy as np
from jax import lax
from jax.experimental import pallas as pl
from jax.experimental.pallas import tpu as pltpu
from jax.sharding import PartitionSpec as P

F32 = jnp.float32
BF16 = jnp.bfloat16
LANES = 128
RADIX = 4


def halves(table):
    high = table.astype(ml_dtypes.bfloat16)
    low = (table - high.astype(np.float64)).astype(ml_dtypes.bfloat16)
    return high, low


def tables(blocks, seq_len):
    slots = blocks // 2
    total = blocks * seq_len
    d = np.arange(blocks)
    s = np.arange(slots)
    m = np.arange(seq_len)
    angle = 2.0 * math.pi / blocks * (s[:, None] * d[None, :] % blocks)
    cos_rows = np.cos(angle)
    sin_rows = np.sin(angle)
    sin_rows[0] = np.where(d % 2 == 0, -1.0, 1.0)
    fwd = np.concatenate([cos_rows, -sin_rows], 0)
    scale = np.where(s == 0, 1.0, 2.0)[:, None] / total
    inv = (fwd * np.concatenate([scale, scale], 0)).T
    turn = 2.0 * math.pi / total * (np.arange(slots + 1)[:, None] * m[None, :] % total)
    twiddle = np.stack([np.cos(turn[:slots]), np.sin(turn[:slots])]).astype(np.float32)
    middle = np.stack([np.cos(turn[slots]), np.sin(turn[slots])]).astype(np.float32)
    middle = np.concatenate([middle, np.zeros((6, seq_len), np.float32)], 0)
    n = np.arange(LANES)[None, :, None]
    l = np.arange(LANES)[None, None, :]
    r = np.arange(RADIX)[:, None, None]
    theta = 2.0 * math.pi / seq_len * (n * (r + RADIX * l) % seq_len)
    cos_t = np.cos(theta)
    sin_t = np.sin(theta)
    dft = np.concatenate(
        [np.concatenate([cos_t, -sin_t], 2), np.concatenate([sin_t, cos_t], 2)], 1
    )
    dft = np.stack([dft, dft.transpose(0, 2, 1)])
    fwd_hl = np.stack(halves(fwd))
    inv_hl = np.stack(halves(inv))
    dft_hl = np.stack(halves(dft), 1)
    return fwd_hl, inv_hl, dft_hl, twiddle, middle


def split(value):
    high = value.astype(BF16)
    return high, (value - high.astype(F32)).astype(BF16)


def mm(left, right):
    return jnp.dot(left, right, preferred_element_type=F32)


def table_dot(table_ref, value):
    high, low = split(value)
    return mm(table_ref[0], high) + mm(table_ref[0], low) + mm(table_ref[1], high)


def radix4(parts, direction):
    (ar, ai), (br, bi), (cr, ci), (dr, di) = parts
    pr, pi, qr, qi = ar + cr, ai + ci, ar - cr, ai - ci
    sr, si, tr, ti = br + dr, bi + di, br - dr, bi - di
    plus = (qr - ti, qi + tr)
    minus = (qr + ti, qi - tr)
    if direction < 0:
        plus, minus = minus, plus
    return (pr + sr, pi + si), plus, (pr - sr, pi - si), minus


def offsets(shape):
    every = [o for o in itertools.product(*[range(n) for n in shape]) if any(o)]
    random.Random(1).shuffle(every)

    def hops(o):
        z, _, x, y = [min(d, n - d) for d, n in zip(o, shape)]
        return z + x + y

    levels = [[], [], []]
    for o in every:
        z, _, x, y = [int(d > 0) for d in o]
        levels[max(z + x + y, 1) - 1].append(o)
    mixed = list(every)
    every.sort(key=lambda o: -hops(o))
    return levels, every, mixed


def kernel(
    shape,
    signal_hbm,
    spectrum_hbm,
    dft_hbm,
    fwd_hbm,
    inv_hbm,
    twiddle_hbm,
    middle_hbm,
    gain_hbm,
    out_ref,
    signal,
    spectrum,
    dft,
    fwd,
    inv,
    twiddle,
    middle,
    gain,
    send_x,
    recv_x,
    send_f,
    recv_f,
    send_y,
    recv_y,
    parts,
    bins,
    back,
    load_sem,
    x_sem,
    f_sem,
    y_sem,
    second_sem,
    third_sem,
):
    n_z, n_core, n_x, n_y = shape
    outer = lax.axis_index("outer")
    inner = lax.axis_index("inner")
    n_outer = n_z * n_core
    n_inner = n_x * n_y
    blocks = n_outer * n_inner
    me = outer * n_inner + inner
    slots = blocks // 2
    seq_len = signal.shape[0]
    m_tiles = seq_len // LANES
    rows = 2 * m_tiles
    lines = bins.shape[2]

    def lanes(tile):
        return pl.ds(tile * LANES, LANES)

    z, core = outer // n_core, lax.rem(outer, n_core)
    x, y = inner // n_y, lax.rem(inner, n_y)
    at_outer = [
        [lax.rem(z + d, n_z) * n_core + lax.rem(core + e, n_core) for e in range(n_core)]
        for d in range(n_z)
    ]
    at_x = [lax.rem(x + d, n_x) * n_y for d in range(n_x)]
    at_y = [lax.rem(y + d, n_y) for d in range(n_y)]
    levels, far, mixed = offsets(shape)

    def device(offset):
        dz, dc, dx, dy = offset
        return at_outer[dz][dc], at_x[dx] + at_y[dy]

    def tell(sem):
        for offset in levels[0]:
            pl.semaphore_signal(
                sem,
                inc=1,
                device_id=device(offset),
                device_id_type=pl.DeviceIdType.MESH,
            )

    def hear(sem):
        pl.semaphore_wait(sem, len(levels[0]))

    barrier = pltpu.get_barrier_semaphore()
    tell(barrier)

    loads = {}

    def load(name, src, dst):
        copy = pltpu.make_async_copy(src, dst, load_sem.at[len(loads)])
        copy.start()
        loads[name] = copy

    for g in range(2):
        for h in range(2):
            where = lanes(2 * h + g)
            load(("x", g, h), signal_hbm.at[:, where], signal.at[:, where])
        load(("f", g), spectrum_hbm.at[:, :, lanes(g)], spectrum.at[g])
    load("fwd", fwd_hbm, fwd)
    load("twiddle", twiddle_hbm, twiddle)
    load("middle", middle_hbm, middle)
    load("dft", dft_hbm, dft)
    load("inv", inv_hbm, inv)
    load("gain", gain_hbm, gain)

    def block(ref, index):
        return ref.at[pl.ds(pl.multiple_of(index * rows, rows), rows)]

    def send(src, dst, sems, order):
        for offset in order:
            to = device(offset)
            pltpu.make_async_remote_copy(
                src_ref=block(src, to[0] * n_inner + to[1]),
                dst_ref=block(dst, me),
                send_sem=sems.at[0],
                recv_sem=sems.at[1],
                device_id=to,
                device_id_type=pl.DeviceIdType.MESH,
            ).start()

    def keep(src, dst):
        own = pl.ds(pl.multiple_of(me * rows, rows), rows)
        dst[own, :] = src[own, :]

    def wait_all(ref, sem):
        part = ref.at[pl.ds(0, (blocks - 1) * rows)]
        pltpu.make_async_copy(part, part, sem).wait()

    def spread(ref, g, index, tile):
        ref[g, pl.ds(index, blocks, stride=rows), :] = tile

    def send_signal(g, order):
        send(send_x.at[g], recv_x.at[g], x_sem.at[g], order)

    def send_filter(g, order):
        send(send_f.at[g], recv_f.at[g], f_sem.at[g], order)

    for g in range(2):
        for h in range(2):
            loads["x", g, h].wait()
            for mt in range(m_tiles):
                spread(send_x, g, h * m_tiles + mt, signal[lanes(mt), lanes(2 * h + g)].T)
        if g == 0:
            hear(barrier)
            tell(second_sem)
        send_signal(g, levels[0])
        loads["f", g].wait()
        for r in range(2):
            for q in range(RADIX):
                every = pl.ds(q, LANES, stride=RADIX)
                spread(send_f, g, r * m_tiles + q, spectrum[g, r, every, :].T)
        send_filter(g, levels[0])
    hear(second_sem)
    tell(third_sem)
    send_signal(0, levels[1])
    send_filter(0, levels[1])
    hear(third_sem)
    send_signal(0, levels[2])
    send_filter(0, levels[2])
    later = [o for o in far if o not in levels[0]]
    send_signal(1, [o for o in mixed if o not in levels[0]])
    send_filter(1, later)
    for g in range(2):
        keep(send_x.at[g], recv_x.at[g])
        keep(send_f.at[g], recv_f.at[g])

    for name in ("fwd", "twiddle", "middle", "dft", "inv", "gain"):
        loads[name].wait()
    first = lax.broadcasted_iota(jnp.int32, (slots, LANES), 0) == 0
    lane = lax.broadcasted_iota(jnp.int32, (1, LANES), 1)
    extra_rows = lines - 2 * slots
    pad = jnp.zeros((extra_rows - 2, LANES), F32)
    tiles = [slice(p * LANES, (p + 1) * LANES) for p in range(RADIX)]

    def put(p, at, count, re, im):
        value = jnp.concatenate([re, im], 1)
        high, low = split(value)
        parts[p, pl.ds(at, count), :] = high
        parts[p, pl.ds(lines + at, count), :] = low

    def transform(p, way):
        whole = mm(parts[p], dft[way, 0, p])
        rest = mm(parts[p, :lines], dft[way, 1, p])
        return whole[:lines] + whole[lines:] + rest

    def forward(g):
        extra = []

        def lines_in(at, count, pairs):
            for p, (re, im) in enumerate(radix4(pairs, -1)):
                put(p, at, count, re, im)

        for h in range(2):
            data = jnp.concatenate(
                [
                    recv_x[g, pl.ds(h * m_tiles + mt, blocks, stride=rows), :]
                    for mt in range(m_tiles)
                ],
                1,
            )
            packed = table_dot(fwd, data)
            extra.append(packed[slots : slots + 1])
            pairs = []
            for t in tiles:
                re = packed[:slots, t]
                im = packed[slots:, t]
                cos_t = twiddle[0, :, t]
                sin_t = twiddle[1, :, t]
                pairs.append(
                    (
                        re * cos_t + im * sin_t,
                        jnp.where(first, 0.0, im * cos_t - re * sin_t),
                    )
                )
            lines_in(h * slots, slots, pairs)
        pairs = []
        for t in tiles:
            value = jnp.concatenate([extra[0][:, t], extra[1][:, t], pad], 0)
            pairs.append((value * middle[0:1, t], -value * middle[1:2, t]))
        lines_in(2 * slots, extra_rows, pairs)
        for p in range(RADIX):
            bins[g, p] = transform(p, 0)

    def times_filter(g, p, at, count, f_re, f_im):
        x_re = bins[g, p, pl.ds(at, count), :LANES]
        x_im = bins[g, p, pl.ds(at, count), LANES:]
        put(p, at, count, f_re * x_re - f_im * x_im, f_re * x_im + f_im * x_re)

    def backward(g):
        lower = lane < LANES // 2
        for p in range(RADIX):
            mid = []
            for h in range(2):
                f_re, f_im = [
                    recv_f[
                        g, pl.ds((h * 2 + r) * m_tiles + p, slots, stride=2 * rows), :
                    ]
                    for r in range(2)
                ]
                top_re = f_re[0:8]
                top_im = f_im[0:8]
                far_re = pltpu.roll(top_re, LANES // 2, 1)[0:1]
                far_im = pltpu.roll(top_im, LANES // 2, 1)[0:1]
                top_re = top_re[0:1]
                top_im = top_im[0:1]
                mid.append(
                    (
                        jnp.where(lower, 2.0 * far_re, 0.0),
                        jnp.where(lower, 2.0 * far_im, 0.0),
                    )
                )
                base_re = jnp.where(lower, 2.0 * top_re, 0.0)
                base_im = jnp.where(lower, 2.0 * top_im, 0.0)
                if p == 0:
                    base_re = jnp.where(lane == 0, top_re, base_re)
                    base_re = jnp.where(lane == LANES // 2, far_im, base_re)
                    base_im = jnp.where(lane == 0, 0.0, base_im)
                times_filter(
                    g,
                    p,
                    h * slots,
                    slots,
                    jnp.where(first, base_re, f_re),
                    jnp.where(first, base_im, f_im),
                )
            times_filter(
                g,
                p,
                2 * slots,
                extra_rows,
                jnp.concatenate([mid[0][0], mid[1][0], pad], 0),
                jnp.concatenate([mid[0][1], mid[1][1], pad], 0),
            )
        for p in range(RADIX):
            back[p] = transform(p, 1)

        def lines_out(at, count):
            at = pl.ds(at, count)
            return radix4([(back[p, at, :LANES], back[p, at, LANES:]) for p in range(RADIX)], 1)

        tail = [
            re * middle[0:1, t] - im * middle[1:2, t]
            for t, (re, im) in zip(tiles, lines_out(2 * slots, extra_rows))
        ]
        for h in range(2):
            v_re = []
            v_im = []
            for t, end, (re, im) in zip(tiles, tail, lines_out(h * slots, slots)):
                cos_t = twiddle[0, :, t]
                sin_t = twiddle[1, :, t]
                v_re.append(re * cos_t - im * sin_t)
                v_im.append(jnp.where(first, end[h : h + 1], re * sin_t + im * cos_t))
            value = jnp.concatenate(
                [jnp.concatenate(v_re, 1), jnp.concatenate(v_im, 1)], 0
            )
            conv = table_dot(inv, value)
            for mt in range(m_tiles):
                spread(send_y, g, h * m_tiles + mt, conv[:, tiles[mt]])

    @pl.loop(0, 2)
    def _(g):
        wait_all(recv_x.at[g], x_sem.at[g, 1])
        forward(g)
        wait_all(recv_f.at[g], f_sem.at[g, 1])
        backward(g)
        for group, order in enumerate((mixed, far)):

            @pl.when(g == group)
            def _():
                send(send_y.at[group], recv_y.at[group], y_sem.at[group], order)

        keep(send_y.at[g], recv_y.at[g])

    for g in range(2):
        wait_all(send_x.at[g], x_sem.at[g, 0])
        wait_all(send_f.at[g], f_sem.at[g, 0])
        wait_all(send_y.at[g], y_sem.at[g, 0])

    for g in range(2):
        wait_all(recv_y.at[g], y_sem.at[g, 1])
        for h in range(2):
            for mt in range(m_tiles):
                tile = recv_y[g, pl.ds(h * m_tiles + mt, blocks, stride=rows), :]
                at = lanes(2 * h + g)
                out_ref[lanes(mt), at] = tile.T + gain[0:1, at] * signal[lanes(mt), at]


def body(signal, spectrum, skip_gain):
    n_outer = lax.axis_size("outer")
    n_inner = lax.axis_size("inner")
    blocks = n_outer * n_inner
    side = math.isqrt(n_inner)
    shape = (n_outer // 2, 2, side, side)
    seq_len, channels = signal.shape
    fwd, inv, dft, twiddle, middle = tables(blocks, seq_len)
    rows = 2 * (seq_len // LANES)
    lines = blocks + 16
    vmem = pltpu.VMEM
    dma = pltpu.SemaphoreType.DMA
    in_hbm = pl.BlockSpec(memory_space=pltpu.HBM)
    return pl.pallas_call(
        functools.partial(kernel, shape),
        out_shape=jax.ShapeDtypeStruct(signal.shape, F32),
        in_specs=[in_hbm] * 8,
        out_specs=pl.BlockSpec(memory_space=pltpu.VMEM),
        scratch_shapes=[
            vmem(signal.shape, F32),
            vmem((2, 2, seq_len, LANES), F32),
            vmem(dft.shape, BF16),
            vmem(fwd.shape, BF16),
            vmem(inv.shape, BF16),
            vmem(twiddle.shape, F32),
            vmem(middle.shape, F32),
            vmem((1, channels), F32),
            *[vmem((2, blocks * rows, LANES), F32) for _ in range(6)],
            vmem((RADIX, 2 * lines, 2 * LANES), BF16),
            vmem((2, RADIX, lines, 2 * LANES), F32),
            vmem((RADIX, lines, 2 * LANES), F32),
            dma((12,)),
            *[dma((2, 2)) for _ in range(3)],
            pltpu.SemaphoreType.REGULAR,
            pltpu.SemaphoreType.REGULAR,
        ],
        compiler_params=pltpu.CompilerParams(
            collective_id=1, has_side_effects=True, vmem_limit_bytes=48 * 2**20
        ),
        cost_estimate=pl.CostEstimate(
            flops=2 * 10**9, bytes_accessed=8 * 2**20, transcendentals=0
        ),
        name="hyena_conv",
    )(
        *[
            pltpu.with_memory_space_constraint(a, pltpu.HBM)
            for a in (
                signal,
                spectrum.reshape(spectrum.shape[1:]),
                dft,
                fwd,
                inv,
                twiddle,
                middle,
                skip_gain[None, :],
            )
        ]
    )


def solution(mesh):
    return jax.shard_map(
        body,
        mesh=mesh,
        in_specs=(P(("outer", "inner"), None), P(("outer", "inner"), None, None, None), P()),
        out_specs=P(("outer", "inner"), None),
        check_vma=False,
    )
```

```python
import functools
import itertools
import math
import random

import jax
import jax.numpy as jnp
import ml_dtypes
import numpy as np
from jax import lax
from jax.experimental import pallas as pl
from jax.experimental.pallas import tpu as pltpu
from jax.sharding import PartitionSpec as P

F32 = jnp.float32
BF16 = jnp.bfloat16
LANES = 128
RADIX = 4


def halves(table):
    high = table.astype(ml_dtypes.bfloat16)
    low = (table - high.astype(np.float64)).astype(ml_dtypes.bfloat16)
    return high, low


def tables(blocks, seq_len):
    slots = blocks // 2
    total = blocks * seq_len
    d = np.arange(blocks)
    s = np.arange(slots)
    m = np.arange(seq_len)
    angle = 2.0 * math.pi / blocks * (s[:, None] * d[None, :] % blocks)
    cos_rows = np.cos(angle)
    sin_rows = np.sin(angle)
    sin_rows[0] = np.where(d % 2 == 0, -1.0, 1.0)
    fwd = np.concatenate([cos_rows, -sin_rows], 0)
    scale = np.where(s == 0, 1.0, 2.0)[:, None] / total
    inv = (fwd * np.concatenate([scale, scale], 0)).T
    turn = 2.0 * math.pi / total * (np.arange(slots + 1)[:, None] * m[None, :] % total)
    twiddle = np.stack([np.cos(turn[:slots]), np.sin(turn[:slots])]).astype(np.float32)
    middle = np.stack([np.cos(turn[slots]), np.sin(turn[slots])]).astype(np.float32)
    middle = np.concatenate([middle, np.zeros((6, seq_len), np.float32)], 0)
    n = np.arange(LANES)[None, :, None]
    l = np.arange(LANES)[None, None, :]
    r = np.arange(RADIX)[:, None, None]
    theta = 2.0 * math.pi / seq_len * (n * (r + RADIX * l) % seq_len)
    cos_t = np.cos(theta)
    sin_t = np.sin(theta)
    dft = np.concatenate(
        [np.concatenate([cos_t, -sin_t], 2), np.concatenate([sin_t, cos_t], 2)], 1
    )
    dft = np.stack([dft, dft.transpose(0, 2, 1)])
    fwd_hl = np.stack(halves(fwd))
    inv_hl = np.stack(halves(inv))
    dft_hl = np.stack(halves(dft), 1)
    return fwd_hl, inv_hl, dft_hl, twiddle, middle


def split(value):
    high = value.astype(BF16)
    return high, (value - high.astype(F32)).astype(BF16)


def mm(left, right):
    return jnp.dot(left, right, preferred_element_type=F32)


def table_dot(table_ref, value):
    high, low = split(value)
    return mm(table_ref[0], high) + mm(table_ref[0], low) + mm(table_ref[1], high)


def radix4(parts, direction):
    (ar, ai), (br, bi), (cr, ci), (dr, di) = parts
    pr, pi, qr, qi = ar + cr, ai + ci, ar - cr, ai - ci
    sr, si, tr, ti = br + dr, bi + di, br - dr, bi - di
    plus = (qr - ti, qi + tr)
    minus = (qr + ti, qi - tr)
    if direction < 0:
        plus, minus = minus, plus
    return (pr + sr, pi + si), plus, (pr - sr, pi - si), minus


def offsets(shape):
    every = [o for o in itertools.product(*[range(n) for n in shape]) if any(o)]
    random.Random(1).shuffle(every)

    def hops(o):
        z, _, x, y = [min(d, n - d) for d, n in zip(o, shape)]
        return z + x + y

    levels = [[], [], []]
    for o in every:
        z, _, x, y = [int(d > 0) for d in o]
        levels[max(z + x + y, 1) - 1].append(o)
    mixed = list(every)
    every.sort(key=lambda o: -hops(o))
    return levels, every, mixed


def kernel(
    shape,
    signal_hbm,
    spectrum_hbm,
    dft_hbm,
    fwd_hbm,
    inv_hbm,
    twiddle_hbm,
    middle_hbm,
    gain_hbm,
    out_ref,
    signal,
    spectrum,
    dft,
    fwd,
    inv,
    twiddle,
    middle,
    gain,
    send_x,
    recv_x,
    send_f,
    recv_f,
    send_y,
    recv_y,
    parts,
    bins,
    back,
    load_sem,
    x_sem,
    f_sem,
    y_sem,
    second_sem,
    third_sem,
):
    n_z, n_core, n_x, n_y = shape
    outer = lax.axis_index("outer")
    inner = lax.axis_index("inner")
    n_outer = n_z * n_core
    n_inner = n_x * n_y
    blocks = n_outer * n_inner
    me = outer * n_inner + inner
    slots = blocks // 2
    seq_len = signal.shape[0]
    m_tiles = seq_len // LANES
    rows = 2 * m_tiles
    lines = bins.shape[2]

    def lanes(tile):
        return pl.ds(tile * LANES, LANES)

    z, core = outer // n_core, lax.rem(outer, n_core)
    x, y = inner // n_y, lax.rem(inner, n_y)
    at_outer = [
        [lax.rem(z + d, n_z) * n_core + lax.rem(core + e, n_core) for e in range(n_core)]
        for d in range(n_z)
    ]
    at_x = [lax.rem(x + d, n_x) * n_y for d in range(n_x)]
    at_y = [lax.rem(y + d, n_y) for d in range(n_y)]
    levels, far, mixed = offsets(shape)

    def device(offset):
        dz, dc, dx, dy = offset
        return at_outer[dz][dc], at_x[dx] + at_y[dy]

    def tell(sem):
        for offset in levels[0]:
            pl.semaphore_signal(
                sem,
                inc=1,
                device_id=device(offset),
                device_id_type=pl.DeviceIdType.MESH,
            )

    def hear(sem):
        pl.semaphore_wait(sem, len(levels[0]))

    barrier = pltpu.get_barrier_semaphore()
    tell(barrier)

    loads = {}

    def load(name, src, dst):
        copy = pltpu.make_async_copy(src, dst, load_sem.at[len(loads)])
        copy.start()
        loads[name] = copy

    for g in range(2):
        for h in range(2):
            where = lanes(2 * h + g)
            load(("x", g, h), signal_hbm.at[:, where], signal.at[:, where])
        load(("f", g), spectrum_hbm.at[:, :, lanes(g)], spectrum.at[g])
    load("fwd", fwd_hbm, fwd)
    load("twiddle", twiddle_hbm, twiddle)
    load("middle", middle_hbm, middle)
    load("dft", dft_hbm, dft)
    load("inv", inv_hbm, inv)
    load("gain", gain_hbm, gain)

    def block(ref, index):
        return ref.at[pl.ds(pl.multiple_of(index * rows, rows), rows)]

    def send(src, dst, sems, order):
        for offset in order:
            to = device(offset)
            pltpu.make_async_remote_copy(
                src_ref=block(src, to[0] * n_inner + to[1]),
                dst_ref=block(dst, me),
                send_sem=sems.at[0],
                recv_sem=sems.at[1],
                device_id=to,
                device_id_type=pl.DeviceIdType.MESH,
            ).start()

    def keep(src, dst):
        own = pl.ds(pl.multiple_of(me * rows, rows), rows)
        dst[own, :] = src[own, :]

    def wait_all(ref, sem):
        part = ref.at[pl.ds(0, (blocks - 1) * rows)]
        pltpu.make_async_copy(part, part, sem).wait()

    def spread(ref, g, index, tile):
        ref[g, pl.ds(index, blocks, stride=rows), :] = tile

    def send_signal(g, order):
        send(send_x.at[g], recv_x.at[g], x_sem.at[g], order)

    def send_filter(g, order):
        send(send_f.at[g], recv_f.at[g], f_sem.at[g], order)

    for g in range(2):
        for h in range(2):
            loads["x", g, h].wait()
            for mt in range(m_tiles):
                spread(send_x, g, h * m_tiles + mt, signal[lanes(mt), lanes(2 * h + g)].T)
        loads["f", g].wait()
        for r in range(2):
            for q in range(RADIX):
                every = pl.ds(q, LANES, stride=RADIX)
                spread(send_f, g, r * m_tiles + q, spectrum[g, r, every, :].T)
    hear(barrier)
    tell(second_sem)
    for g in range(2):
        send_signal(g, levels[0])
        send_filter(g, levels[0])
    hear(second_sem)
    tell(third_sem)
    send_signal(0, levels[1])
    send_filter(0, levels[1])
    hear(third_sem)
    send_signal(0, levels[2])
    send_filter(0, levels[2])
    later = [o for o in far if o not in levels[0]]
    send_signal(1, [o for o in mixed if o not in levels[0]])
    send_filter(1, later)
    for g in range(2):
        keep(send_x.at[g], recv_x.at[g])
        keep(send_f.at[g], recv_f.at[g])

    for name in ("fwd", "twiddle", "middle", "dft", "inv", "gain"):
        loads[name].wait()
    first = lax.broadcasted_iota(jnp.int32, (slots, LANES), 0) == 0
    lane = lax.broadcasted_iota(jnp.int32, (1, LANES), 1)
    extra_rows = lines - 2 * slots
    pad = jnp.zeros((extra_rows - 2, LANES), F32)
    tiles = [slice(p * LANES, (p + 1) * LANES) for p in range(RADIX)]

    def put(p, at, count, re, im):
        value = jnp.concatenate([re, im], 1)
        high, low = split(value)
        parts[p, pl.ds(at, count), :] = high
        parts[p, pl.ds(lines + at, count), :] = low

    def transform(p, way):
        whole = mm(parts[p], dft[way, 0, p])
        rest = mm(parts[p, :lines], dft[way, 1, p])
        return whole[:lines] + whole[lines:] + rest

    def forward(g):
        extra = []

        def lines_in(at, count, pairs):
            for p, (re, im) in enumerate(radix4(pairs, -1)):
                put(p, at, count, re, im)

        for h in range(2):
            data = jnp.concatenate(
                [
                    recv_x[g, pl.ds(h * m_tiles + mt, blocks, stride=rows), :]
                    for mt in range(m_tiles)
                ],
                1,
            )
            packed = table_dot(fwd, data)
            extra.append(packed[slots : slots + 1])
            pairs = []
            for t in tiles:
                re = packed[:slots, t]
                im = packed[slots:, t]
                cos_t = twiddle[0, :, t]
                sin_t = twiddle[1, :, t]
                pairs.append(
                    (
                        re * cos_t + im * sin_t,
                        jnp.where(first, 0.0, im * cos_t - re * sin_t),
                    )
                )
            lines_in(h * slots, slots, pairs)
        pairs = []
        for t in tiles:
            value = jnp.concatenate([extra[0][:, t], extra[1][:, t], pad], 0)
            pairs.append((value * middle[0:1, t], -value * middle[1:2, t]))
        lines_in(2 * slots, extra_rows, pairs)
        for p in range(RADIX):
            bins[g, p] = transform(p, 0)

    def times_filter(g, p, at, count, f_re, f_im):
        x_re = bins[g, p, pl.ds(at, count), :LANES]
        x_im = bins[g, p, pl.ds(at, count), LANES:]
        put(p, at, count, f_re * x_re - f_im * x_im, f_re * x_im + f_im * x_re)

    def backward(g):
        lower = lane < LANES // 2
        for p in range(RADIX):
            mid = []
            for h in range(2):
                f_re, f_im = [
                    recv_f[
                        g, pl.ds((h * 2 + r) * m_tiles + p, slots, stride=2 * rows), :
                    ]
                    for r in range(2)
                ]
                top_re = f_re[0:8]
                top_im = f_im[0:8]
                far_re = pltpu.roll(top_re, LANES // 2, 1)[0:1]
                far_im = pltpu.roll(top_im, LANES // 2, 1)[0:1]
                top_re = top_re[0:1]
                top_im = top_im[0:1]
                mid.append(
                    (
                        jnp.where(lower, 2.0 * far_re, 0.0),
                        jnp.where(lower, 2.0 * far_im, 0.0),
                    )
                )
                base_re = jnp.where(lower, 2.0 * top_re, 0.0)
                base_im = jnp.where(lower, 2.0 * top_im, 0.0)
                if p == 0:
                    base_re = jnp.where(lane == 0, top_re, base_re)
                    base_re = jnp.where(lane == LANES // 2, far_im, base_re)
                    base_im = jnp.where(lane == 0, 0.0, base_im)
                times_filter(
                    g,
                    p,
                    h * slots,
                    slots,
                    jnp.where(first, base_re, f_re),
                    jnp.where(first, base_im, f_im),
                )
            times_filter(
                g,
                p,
                2 * slots,
                extra_rows,
                jnp.concatenate([mid[0][0], mid[1][0], pad], 0),
                jnp.concatenate([mid[0][1], mid[1][1], pad], 0),
            )
        for p in range(RADIX):
            back[p] = transform(p, 1)

        def lines_out(at, count):
            at = pl.ds(at, count)
            return radix4([(back[p, at, :LANES], back[p, at, LANES:]) for p in range(RADIX)], 1)

        tail = [
            re * middle[0:1, t] - im * middle[1:2, t]
            for t, (re, im) in zip(tiles, lines_out(2 * slots, extra_rows))
        ]
        for h in range(2):
            v_re = []
            v_im = []
            for t, end, (re, im) in zip(tiles, tail, lines_out(h * slots, slots)):
                cos_t = twiddle[0, :, t]
                sin_t = twiddle[1, :, t]
                v_re.append(re * cos_t - im * sin_t)
                v_im.append(jnp.where(first, end[h : h + 1], re * sin_t + im * cos_t))
            value = jnp.concatenate(
                [jnp.concatenate(v_re, 1), jnp.concatenate(v_im, 1)], 0
            )
            conv = table_dot(inv, value)
            for mt in range(m_tiles):
                spread(send_y, g, h * m_tiles + mt, conv[:, tiles[mt]])

    for g in range(2):
        wait_all(recv_x.at[g], x_sem.at[g, 1])
        forward(g)
        wait_all(recv_f.at[g], f_sem.at[g, 1])
        backward(g)
        send(send_y.at[g], recv_y.at[g], y_sem.at[g], (mixed, far)[g])
        keep(send_y.at[g], recv_y.at[g])

    for g in range(2):
        wait_all(send_x.at[g], x_sem.at[g, 0])
        wait_all(send_f.at[g], f_sem.at[g, 0])
        wait_all(send_y.at[g], y_sem.at[g, 0])

    for g in range(2):
        wait_all(recv_y.at[g], y_sem.at[g, 1])
        for h in range(2):
            for mt in range(m_tiles):
                tile = recv_y[g, pl.ds(h * m_tiles + mt, blocks, stride=rows), :]
                at = lanes(2 * h + g)
                out_ref[lanes(mt), at] = tile.T + gain[0:1, at] * signal[lanes(mt), at]


def body(signal, spectrum, skip_gain):
    n_outer = lax.axis_size("outer")
    n_inner = lax.axis_size("inner")
    blocks = n_outer * n_inner
    side = math.isqrt(n_inner)
    shape = (n_outer // 2, 2, side, side)
    seq_len, channels = signal.shape
    fwd, inv, dft, twiddle, middle = tables(blocks, seq_len)
    rows = 2 * (seq_len // LANES)
    lines = blocks + 16
    vmem = pltpu.VMEM
    dma = pltpu.SemaphoreType.DMA
    in_hbm = pl.BlockSpec(memory_space=pltpu.HBM)
    return pl.pallas_call(
        functools.partial(kernel, shape),
        out_shape=jax.ShapeDtypeStruct(signal.shape, F32),
        in_specs=[in_hbm] * 8,
        out_specs=pl.BlockSpec(memory_space=pltpu.VMEM),
        scratch_shapes=[
            vmem(signal.shape, F32),
            vmem((2, 2, seq_len, LANES), F32),
            vmem(dft.shape, BF16),
            vmem(fwd.shape, BF16),
            vmem(inv.shape, BF16),
            vmem(twiddle.shape, F32),
            vmem(middle.shape, F32),
            vmem((1, channels), F32),
            *[vmem((2, blocks * rows, LANES), F32) for _ in range(6)],
            vmem((RADIX, 2 * lines, 2 * LANES), BF16),
            vmem((2, RADIX, lines, 2 * LANES), F32),
            vmem((RADIX, lines, 2 * LANES), F32),
            dma((12,)),
            *[dma((2, 2)) for _ in range(3)],
            pltpu.SemaphoreType.REGULAR,
            pltpu.SemaphoreType.REGULAR,
        ],
        compiler_params=pltpu.CompilerParams(
            collective_id=1, has_side_effects=True, vmem_limit_bytes=48 * 2**20
        ),
        cost_estimate=pl.CostEstimate(
            flops=2 * 10**9, bytes_accessed=8 * 2**20, transcendentals=0
        ),
        name="hyena_conv",
    )(
        *[
            pltpu.with_memory_space_constraint(a, pltpu.HBM)
            for a in (
                signal,
                spectrum.reshape(spectrum.shape[1:]),
                dft,
                fwd,
                inv,
                twiddle,
                middle,
                skip_gain[None, :],
            )
        ]
    )


def solution(mesh):
    return jax.shard_map(
        body,
        mesh=mesh,
        in_specs=(P(("outer", "inner"), None), P(("outer", "inner"), None, None, None), P()),
        out_specs=P(("outer", "inner"), None),
        check_vma=False,
    )
```
